32 devices in a mesh: dp: 8 (over z, x), frame: 4 (over y, core).
Axes of the slice: x: 2, y: 2, z: 4, core: 2. Of those that a mesh axis runs over, the one named last changes fastest.
Arguments:
- features: bfloat16 [8, 16, 32, 64, 128], P('dp', 'frame'), may hold values from -6 to 6
- vis_block: int32 [8, 8, 16, 2], P('dp', None, 'frame'), may hold values from 0 to 31
- vis_count: int32 [8, 8, 16], P('dp', None, 'frame'), may hold values from 1 to 2
- query_frame: int32 [8, 128], P('dp'), may hold values from 0 to 15
- query_block: int32 [8, 128], P('dp'), may hold values from 0 to 31
- query_cell: int32 [8, 128], P('dp'), may hold values from 0 to 63
- cotangent: bfloat16 [8, 4, 128, 16], P('dp', None, 'frame')
- w_in: bfloat16 [128, 384], replicated, may hold values from -0.5 to 0.5
- gain: float32 [384], replicated, may hold values from 0.1 to 1.9
- w_qkv: bfloat16 [384, 1152], replicated, may hold values from -0.3125 to 0.3125
- w_out: bfloat16 [384, 384], replicated, may hold values from -0.3125 to 0.3125
- w_head: bfloat16 [4, 384], replicated, may hold values from -0.3125 to 0.3125
Outputs:
- grad_in: float32 [128, 384], replicated
- grad_gain: float32 [384], replicated
- grad_qkv: float32 [384, 1152], replicated
- grad_out: float32 [384, 384], replicated
- grad_head: float32 [4, 384], replicated
The draws below stay inside these ranges and needn't reach their ends.
Inputs may be any that keep to these rules, and one draw needn't show every extreme that they name: vis_count counts the leading visible slots of vis_block.
All inputs are finite; a program needn't handle non-finite values.
Results may differ from the reference program's by a relative error of at most 0.012.
Values may be sent and summed in bfloat16 or wider, within the bound.
A program may use at most 64 MiB of HBM per device.

```python
import math
import jax
import jax.numpy as jnp
from jax import lax

C = 128
HID = 384
HEADS = 8
FRAMES = 16
P_SIZE = 64
KB = 2
CORR = 128
OUTD = 4
TG = 16
NB = 32
GROUPS = 8
TRACKS = 128
CLIPS = 8


def draw_cotangent(key, part):
    first = jax.random.fold_in(jax.random.fold_in(key, 17), 0)
    shape = (CLIPS, OUTD, TRACKS, FRAMES)
    rising = 1.0 + 2.0 * jnp.arange(CLIPS, dtype=jnp.float32) / max(CLIPS - 1, 1)
    rising = rising[:, None, None, None]
    base = jax.random.normal(first, shape, jnp.float32)
    factor = 1.0 / math.sqrt(CLIPS * TRACKS * FRAMES)
    return (base * rising * factor).astype(jnp.bfloat16)


def plant(result, key, low, high):
    shape = result.shape
    index_at = [jax.random.randint(jax.random.fold_in(key, axis), (), 0, shape[axis]) for axis in range(len(shape))]
    result = result.at[tuple(index_at)].set(low)
    longest = shape.index(max(shape))
    index_at[longest] = (index_at[longest] + 1) % shape[longest]
    return result.at[tuple(index_at)].set(high)


def block_levels(key, extent, shards, smallest, high):
    def one(dim, shards_of):
        draws = jax.random.uniform(jax.random.fold_in(jax.random.fold_in(key, 6), dim), (shards_of,), jnp.float32, smallest / len(shards), high / len(shards))
        return jnp.repeat(jnp.exp(draws), extent[dim] // shards_of).reshape((-1,) + (1,) * (len(extent) - dim - 1))

    level = one(*shards[0])
    for cut in shards[1:]:
        level = level * one(*cut)
    return level


def gaussian(key, dims, scale, limit, cuts=(), kind=jnp.bfloat16):
    loudness = block_levels(key, dims, cuts, -0.22, 0.18) if cuts else 1.0
    array = jax.random.normal(key, dims, jnp.float32) * scale * loudness
    return jnp.minimum(jnp.maximum(array, -limit), limit).astype(kind)


def setup_inputs(seed: int = 0) -> dict:
    key_of = jax.random.split(jax.random.key(seed), 13)
    features = gaussian(key_of[0], (CLIPS, FRAMES, NB, P_SIZE, C), 1.0, 6.0, ((0, 8), (1, 4)))
    vis_block = plant(jax.random.randint(key_of[1], (CLIPS, GROUPS, FRAMES, KB), 0, NB), jax.random.fold_in(key_of[1], 1), 0, NB - 1).astype(jnp.int32)
    vis_count = plant(jax.random.randint(key_of[2], (CLIPS, GROUPS, FRAMES), 1, KB + 1), jax.random.fold_in(key_of[2], 1), 1, KB).astype(jnp.int32)
    query_frame = plant(jax.random.randint(key_of[3], (CLIPS, TRACKS), 0, FRAMES), jax.random.fold_in(key_of[3], 1), 0, FRAMES - 1).astype(jnp.int32)
    query_block = plant(jax.random.randint(key_of[4], (CLIPS, TRACKS), 0, NB), jax.random.fold_in(key_of[4], 1), 0, NB - 1).astype(jnp.int32)
    query_cell = plant(jax.random.randint(key_of[5], (CLIPS, TRACKS), 0, P_SIZE), jax.random.fold_in(key_of[5], 1), 0, P_SIZE - 1).astype(jnp.int32)
    cotangent = draw_cotangent(jax.random.fold_in(key_of[12], 71), 0)
    w_in = gaussian(key_of[7], (CORR, HID), CORR ** -0.5, 0.5)
    gain = jnp.clip(1.0 + 0.18 * jax.random.normal(key_of[8], (HID,), jnp.float32), 0.1, 1.9)
    w_qkv = gaussian(key_of[9], (HID, 3 * HID), HID ** -0.5, 0.3125)
    w_out = gaussian(key_of[10], (HID, HID), HID ** -0.5, 0.3125)
    w_head = gaussian(key_of[11], (OUTD, HID), HID ** -0.5, 0.3125)
    return {"features": features, "vis_block": vis_block, "vis_count": vis_count, "query_frame": query_frame, "query_block": query_block, "query_cell": query_cell, "cotangent": cotangent, "w_in": w_in, "gain": gain, "w_qkv": w_qkv, "w_out": w_out, "w_head": w_head}


def attend(query, keys, values):
    scale = query.shape[-1] ** (-0.5)
    scores = jnp.einsum('nfhd,nghd->nhfg', query.astype(jnp.float32), keys.astype(jnp.float32)) * scale
    probs = jax.nn.softmax(scores, axis=-1).astype(jnp.bfloat16)
    probs = lax.optimization_barrier(probs)
    mixed = jnp.einsum('nhfg,nghd->nfhd', probs.astype(jnp.float32), values.astype(jnp.float32))
    return mixed.astype(jnp.bfloat16)

def local_grads(corr, cot, w_in, gain, w_qkv, w_out, w_head):
    tracks, frames, width = corr.shape
    total = tracks * frames
    hid = w_in.shape[1]
    head_size = hid // HEADS
    rows = corr.reshape(total, width)
    x_zero = jnp.dot(rows, w_in, preferred_element_type=jnp.float32)
    centred = x_zero - lax.optimization_barrier(jnp.mean(x_zero, axis=-1, keepdims=True))
    inv_std = lax.rsqrt(lax.optimization_barrier(jnp.mean(centred * centred, axis=-1, keepdims=True)) + 1e-05)
    normed = centred * inv_std
    hidden = (normed * gain).astype(jnp.bfloat16)
    qkv = jnp.dot(hidden, w_qkv, preferred_element_type=jnp.float32).astype(jnp.bfloat16)
    split = qkv.reshape(tracks, frames, 3, HEADS, head_size)
    mixed, backward = jax.vjp(attend, split[:, :, 0], split[:, :, 1], split[:, :, 2])
    mixed = mixed.reshape(total, hid)
    y_out = (x_zero + jnp.dot(mixed, w_out, preferred_element_type=jnp.float32)).astype(jnp.bfloat16)
    ct_rows = cot.reshape(cot.shape[0], total)
    g_head = jnp.dot(ct_rows, y_out, preferred_element_type=jnp.float32)
    d_y = jnp.dot(ct_rows.T, w_head, preferred_element_type=jnp.float32)
    d_y16 = d_y.astype(jnp.bfloat16)
    g_out = jnp.dot(mixed.T, d_y16, preferred_element_type=jnp.float32)
    d_mixed = jnp.dot(d_y16, w_out.T, preferred_element_type=jnp.float32).astype(jnp.bfloat16)
    d_q, d_k, d_v = backward(d_mixed.reshape(tracks, frames, HEADS, head_size))
    d_qkv = jnp.stack([d_q, d_k, d_v], axis=2).reshape(total, 3 * hid)
    g_qkv = jnp.dot(hidden.T, d_qkv, preferred_element_type=jnp.float32)
    d_hidden = jnp.dot(d_qkv, w_qkv.T, preferred_element_type=jnp.float32)
    g_gain = lax.optimization_barrier(jnp.sum(d_hidden * normed, axis=0))
    d_norm = d_hidden * gain
    d_x = inv_std * (d_norm - lax.optimization_barrier(jnp.mean(d_norm, axis=-1, keepdims=True)) - normed * lax.optimization_barrier(jnp.mean(d_norm * normed, axis=-1, keepdims=True))) + d_y
    d_x16 = d_x.astype(jnp.bfloat16)
    g_in = jnp.dot(rows.T, d_x16, preferred_element_type=jnp.float32)
    return (g_in, g_gain, g_qkv, g_out, g_head)

def correlate(feats, blocks, counts, q_frame, q_block, q_cell):
    query = feats[q_frame, q_block, q_cell]
    frame_ids = jnp.arange(FRAMES, dtype=jnp.int32)[None, :, None]
    patches = feats[frame_ids, blocks]
    live = jnp.arange(KB, dtype=jnp.int32)[None, None, :] < counts[:, :, None]
    patches = jnp.where(live[..., None, None], patches, jnp.zeros((), jnp.bfloat16))
    corr = jnp.einsum('gtc,gfkpc->gtfkp', query.reshape(GROUPS, TG, C).astype(jnp.float32), patches.astype(jnp.float32))
    corr = (corr * C ** (-0.5)).astype(jnp.bfloat16)
    return corr.reshape(TRACKS, FRAMES, KB * P_SIZE)

def reference(features, vis_block, vis_count, query_frame, query_block, query_cell, cotangent, w_in, gain, w_qkv, w_out, w_head):

    def per_clip(total, items):
        feats, blocks, counts, q_frame, q_block, q_cell, cot = items
        corr = correlate(feats, blocks, counts, q_frame, q_block, q_cell)
        grads = local_grads(corr, cot, w_in, gain, w_qkv, w_out, w_head)
        return (jax.tree.map(lambda a, b: a + b, total, grads), None)
    zeros = (jnp.zeros((KB * P_SIZE, HID), jnp.float32), jnp.zeros((HID,), jnp.float32), jnp.zeros((HID, 3 * HID), jnp.float32), jnp.zeros((HID, HID), jnp.float32), jnp.zeros((OUTD, HID), jnp.float32))
    summed, _ = lax.scan(per_clip, zeros, (features, vis_block, vis_count, query_frame, query_block, query_cell, cotangent))
    return (summed[0], summed[1], summed[2], summed[3], summed[4])
```

```python
import functools

import jax
import jax.numpy as jnp
from jax import lax
from jax.experimental import pallas as pl
from jax.experimental.pallas import tpu as pltpu
from jax.sharding import PartitionSpec as P

HEADS = 8
LANES = 128
SUB = 8
PACK = 16
MESH = pl.DeviceIdType.MESH
F32 = jnp.float32
BF16 = jnp.bfloat16


def dot_nn(left, right):
    return lax.dot_general(left, right, (((1,), (0,)), ((), ())), preferred_element_type=F32)


def dot_nt(left, right):
    return lax.dot_general(left, right, (((1,), (1,)), ((), ())), preferred_element_type=F32)


def dot_tn(left, right):
    return lax.dot_general(left, right, (((0,), (0,)), ((), ())), preferred_element_type=F32)


def pick_kernel(feats, vis_block, vis_count, q_frame, q_block, q_cell, queries, patches, picked):
    fr_dev, cells, width = feats.shape[1], feats.shape[3], feats.shape[4]
    groups, slots = vis_block.shape[1], vis_block.shape[3]
    tracks = q_frame.shape[1]
    first = lax.axis_index("frame") * fr_dev
    row_id = lax.broadcasted_iota(jnp.int32, (PACK, width), 0)

    @pl.loop(0, tracks // SUB)
    def _(step):
        for i in range(SUB):
            t = step * SUB + i
            local = q_frame[0, t] - first
            cell = q_cell[0, t]
            base = pl.multiple_of(lax.div(cell, PACK) * PACK, PACK)
            inside = jnp.logical_and(local >= 0, local < fr_dev)
            row = jnp.where(inside, lax.rem(cell, PACK), PACK)
            tile = feats[0, jnp.clip(local, 0, fr_dev - 1), q_block[0, t], pl.ds(base, PACK), :]
            kept = jnp.where(row_id == row, tile.astype(F32), 0.0)
            picked[pl.ds(t, 1), :] = jnp.sum(kept, axis=0, keepdims=True)

    queries[...] = picked[...].astype(BF16)
    for g in range(groups):
        for f in range(fr_dev):
            for k in range(slots):
                patch = feats[0, f, vis_block[0, g, f, k]]
                live = k < vis_count[0, g, f]
                patches[g, f, k * cells : (k + 1) * cells] = jnp.where(
                    live, patch, jnp.zeros_like(patch)
                )


def pick(feats, vis_block, vis_count, q_frame, q_block, q_cell):
    fr_dev, cells, width = feats.shape[1], feats.shape[3], feats.shape[4]
    groups, slots = vis_block.shape[1], vis_block.shape[3]
    tracks = q_frame.shape[1]
    smem = pl.BlockSpec(memory_space=pltpu.SMEM)
    vmem = pl.BlockSpec(memory_space=pltpu.VMEM)
    return pl.pallas_call(
        pick_kernel,
        out_shape=[
            jax.ShapeDtypeStruct((tracks, width), BF16),
            jax.ShapeDtypeStruct((groups, fr_dev, slots * cells, width), BF16),
        ],
        in_specs=[vmem] + [smem] * 5,
        out_specs=[vmem, vmem],
        scratch_shapes=[pltpu.VMEM((tracks, width), F32)],
        compiler_params=pltpu.CompilerParams(vmem_limit_bytes=32 * 2**20),
        name="pick",
    )(feats, vis_block, vis_count, q_frame, q_block, q_cell)


def corr_kernel(n, picked, patches, out, q_recv, c_send, q_ssem, q_rsem, c_ssem, c_rsem):
    me = lax.axis_index("frame")
    groups, fr_dev, _, width = patches.shape
    in_group = picked.shape[0] // groups
    own = groups // n
    barrier = pltpu.get_barrier_semaphore()
    for j in range(1, n):
        pl.semaphore_signal(
            barrier, inc=1, device_id={"frame": lax.rem(me + j, n)}, device_id_type=MESH
        )
    pl.semaphore_wait(barrier, n - 1)
    copies = []
    for j in range(1, n):
        copy = pltpu.make_async_remote_copy(
            src_ref=picked,
            dst_ref=q_recv.at[j - 1],
            send_sem=q_ssem.at[j - 1],
            recv_sem=q_rsem.at[j - 1],
            device_id={"frame": lax.rem(me + j, n)},
            device_id_type=MESH,
        )
        copy.start()
        copies.append(copy)
    for copy in copies:
        copy.wait()
    total = picked[...].astype(F32)
    for j in range(1, n):
        total = total + q_recv[j - 1].astype(F32)
    query = total.astype(BF16)

    scale = width ** (-0.5)
    for g in range(groups):
        q_rows = query[g * in_group : (g + 1) * in_group]
        for f in range(fr_dev):
            corr = dot_nt(q_rows, patches[g, f]) * scale
            c_send[g // own, g % own, f] = corr.astype(BF16)
    copies = []
    for j in range(1, n):
        peer = lax.rem(me + j, n)
        copy = pltpu.make_async_remote_copy(
            src_ref=c_send.at[peer],
            dst_ref=out.at[me],
            send_sem=c_ssem.at[j - 1],
            recv_sem=c_rsem.at[j - 1],
            device_id={"frame": peer},
            device_id_type=MESH,
        )
        copy.start()
        copies.append(copy)
    out[me] = c_send[me]
    for copy in copies:
        copy.wait()


def correlate(n, picked, patches):
    groups, fr_dev, cells, _ = patches.shape
    tracks, width = picked.shape
    shape = (n, groups // n, fr_dev, tracks // groups, cells)
    vmem = pl.BlockSpec(memory_space=pltpu.VMEM)
    sems = pltpu.SemaphoreType.DMA((n - 1,))
    return pl.pallas_call(
        functools.partial(corr_kernel, n),
        out_shape=jax.ShapeDtypeStruct(shape, BF16),
        in_specs=[vmem, vmem],
        out_specs=vmem,
        scratch_shapes=[
            pltpu.VMEM((n - 1, tracks, width), BF16),
            pltpu.VMEM(shape, BF16),
            sems,
            sems,
            sems,
            sems,
        ],
        compiler_params=pltpu.CompilerParams(
            collective_id=0, has_side_effects=True, vmem_limit_bytes=32 * 2**20
        ),
        name="correlate",
    )(picked, patches)


def layer_kernel(corr, ct, w_in, gain, w_qkv, w_out, w_head, packed, head_pad, qkv_t, dqkv_t, att_t, datt_t):
    n, own, fr_dev, in_group, width = corr.shape
    frames = n * fr_dev
    hid = w_in.shape[1]
    size = hid // HEADS
    block = frames * SUB
    halves = in_group // SUB
    tokens = own * halves * block

    c32 = corr[...].astype(F32)
    parts = []
    for g in range(own):
        piece = c32[:, g].reshape(frames, halves, SUB, width)
        for half in range(halves):
            parts.append(piece[:, half].reshape(block, width))
    rows32 = jnp.concatenate(parts, axis=0)
    rows = rows32.astype(BF16)
    rows_t = rows32.T.astype(BF16)

    x_zero = dot_nn(w_in[...].T, rows_t)
    centred = x_zero - jnp.mean(x_zero, axis=0, keepdims=True)
    inv_std = lax.rsqrt(jnp.mean(centred * centred, axis=0, keepdims=True) + 1e-05)
    normed = centred * inv_std
    gain_col = gain[...]
    hidden = (normed * gain_col).astype(BF16)
    qkv_t[...] = dot_nn(w_qkv[...].T, hidden).astype(BF16)

    head_pad[...] = jnp.zeros_like(head_pad)
    head_pad[0 : w_head.shape[0], :] = w_head[...].astype(F32)
    ct_rows = ct[...]
    d_y = dot_tn(head_pad[...].astype(BF16), ct_rows)
    d_y16 = d_y.astype(BF16)
    datt_t[...] = dot_nn(w_out[...], d_y16).astype(BF16)

    scale = size ** (-0.5)
    key_id = lax.broadcasted_iota(jnp.int32, (block, block), 0)
    query_id = lax.broadcasted_iota(jnp.int32, (block, block), 1)
    same = lax.rem(key_id, SUB) == lax.rem(query_id, SUB)
    to_exp2 = scale * 1.4426950408889634

    for b in range(tokens // block):
        at = pl.ds(b * block, block)
        for head in range(HEADS):
            mine = pl.ds(head * size, size)
            q = qkv_t[mine, at]
            k = qkv_t[pl.ds(hid + head * size, size), at]
            v = qkv_t[pl.ds(2 * hid + head * size, size), at]
            d_att = datt_t[mine, at]
            scores = jnp.where(same, dot_tn(k, q), -1e30)
            top = jnp.max(scores, axis=0, keepdims=True)
            powers = jnp.exp2((scores - top) * to_exp2)
            probs = powers * (1.0 / jnp.sum(powers, axis=0, keepdims=True))
            probs16 = probs.astype(BF16)
            att_t[mine, at] = dot_nn(v, probs16).astype(BF16)
            d_v = dot_nt(d_att, probs16)
            d_probs = dot_tn(v, d_att).astype(BF16).astype(F32)
            weighted = probs * d_probs
            d_scores = weighted - probs * jnp.sum(weighted, axis=0, keepdims=True)
            d_scores = d_scores.astype(BF16)
            d_q = dot_nn(k, d_scores) * scale
            d_k = dot_nt(q, d_scores) * scale
            dqkv_t[mine, at] = d_q.astype(BF16)
            dqkv_t[pl.ds(hid + head * size, size), at] = d_k.astype(BF16)
            dqkv_t[pl.ds(2 * hid + head * size, size), at] = d_v.astype(BF16)

    def put(row, value):
        for tile in range(value.shape[1] // LANES):
            packed[pl.ds(row, value.shape[0]), :] = value[
                :, tile * LANES : (tile + 1) * LANES
            ].astype(BF16)
            row += value.shape[0]
        return row

    att = att_t[...]
    y_out = (x_zero + dot_nn(w_out[...].T, att)).astype(BF16)
    d_qkv = dqkv_t[...]
    d_hidden = dot_nn(w_qkv[...], d_qkv)
    product = d_hidden * normed
    d_norm = d_hidden * gain_col
    d_x = (
        inv_std
        * (
            d_norm
            - jnp.mean(d_norm, axis=0, keepdims=True)
            - normed * jnp.mean(d_norm * normed, axis=0, keepdims=True)
        )
        + d_y
    )
    row = put(0, dot_nt(rows_t, d_x.astype(BF16)))
    row = put(row, dot_nt(hidden, d_qkv))
    row = put(row, dot_nt(att, d_y16))
    high = product.astype(BF16)
    low = (product - high.astype(F32)).astype(BF16)
    picks = (lax.broadcasted_iota(jnp.int32, (PACK, tokens), 0) == SUB).astype(F32).astype(BF16)
    row = put(row, dot_nt(ct_rows, y_out) + dot_nt(picks, high) + dot_nt(picks, low))
    if row < packed.shape[0]:
        packed[pl.ds(row, packed.shape[0] - row), :] = jnp.zeros(
            (packed.shape[0] - row, LANES), BF16
        )


def packed_rows(shapes, devices):
    rows = sum(-(-r // PACK) * PACK * (c // LANES) for r, c in shapes)
    step = PACK * devices
    return -(-rows // step) * step


def layer(rows, corr, ct, w_in, gain, w_qkv, w_out, w_head):
    hid = w_in.shape[1]
    tokens = ct.shape[1]
    vmem = pl.BlockSpec(memory_space=pltpu.VMEM)
    return pl.pallas_call(
        layer_kernel,
        out_shape=jax.ShapeDtypeStruct((rows, LANES), BF16),
        in_specs=[vmem] * 7,
        out_specs=vmem,
        scratch_shapes=[
            pltpu.VMEM((PACK, hid), F32),
            pltpu.VMEM((3 * hid, tokens), BF16),
            pltpu.VMEM((3 * hid, tokens), BF16),
            pltpu.VMEM((hid, tokens), BF16),
            pltpu.VMEM((hid, tokens), BF16),
        ],
        compiler_params=pltpu.CompilerParams(vmem_limit_bytes=48 * 2**20),
        name="layer",
    )(corr, ct, w_in, gain, w_qkv, w_out, w_head)


def factors(dp, frame):
    core = 2 if frame % 2 == 0 else 1
    mid = frame // core
    low = mid if dp % mid == 0 else 1
    return core, mid, low, dp // low


def stages(dp, frame):
    n_core, n_y, n_x, n_z = factors(dp, frame)
    me_d, me_f = lax.axis_index("dp"), lax.axis_index("frame")
    core, y = lax.rem(me_f, n_core), lax.div(me_f, n_core)
    x, z = lax.rem(me_d, n_x), lax.div(me_d, n_x)
    swap = core if n_core == 2 and n_x == n_y else 0

    def device(core_at, y_at, x_at, z_at):
        return (z_at * n_x + x_at, y_at * n_core + core_at)

    keep = 1 - swap
    return (
        (n_core, core, lambda d: device(d, y, x, z)),
        (n_x, keep * x + swap * y, lambda d: device(core, keep * y + swap * d, keep * d + swap * x, z)),
        (n_y, keep * y + swap * x, lambda d: device(core, keep * d + swap * y, keep * x + swap * d, z)),
        (n_z, z, lambda d: device(core, y, x, d)),
    )


def sum_kernel(dp, frame, given, out, work, r0, r1, r2, r3, *sems):
    plan = stages(dp, frame)
    recvs = (r0, r1, r2, r3)
    barrier = pltpu.get_barrier_semaphore()
    peers = 0
    for size, digit, device in plan:
        for j in range(1, size):
            pl.semaphore_signal(
                barrier, inc=1, device_id=device(lax.rem(digit + j, size)), device_id_type=MESH
            )
            peers += 1
    pl.semaphore_wait(barrier, peers)

    begin, count = 0, given.shape[0]
    for at, (size, digit, device) in enumerate(plan):
        source = given if at == 0 else work
        target = out if at == len(plan) - 1 else work
        part = count // size
        copies = []
        for j in range(1, size):
            peer = lax.rem(digit + j, size)
            copy = pltpu.make_async_remote_copy(
                src_ref=source.at[pl.ds(pl.multiple_of(begin + peer * part, PACK), part)],
                dst_ref=recvs[at].at[j - 1],
                send_sem=sems[4 * at].at[j - 1],
                recv_sem=sems[4 * at + 1].at[j - 1],
                device_id=device(peer),
                device_id_type=MESH,
            )
            copy.start()
            copies.append(copy)
        for copy in copies:
            copy.wait()
        begin = pl.multiple_of(begin + digit * part, PACK)
        count = part
        total = source[pl.ds(begin, part), :].astype(F32)
        for j in range(1, size):
            total = total + recvs[at][j - 1].astype(F32)
        target[pl.ds(begin, part), :] = total.astype(BF16)

    for at in reversed(range(len(plan))):
        size, digit, device = plan[at]
        copies = []
        for j in range(1, size):
            here = out.at[pl.ds(begin, count)]
            copy = pltpu.make_async_remote_copy(
                src_ref=here,
                dst_ref=here,
                send_sem=sems[4 * at + 2].at[j - 1],
                recv_sem=sems[4 * at + 3].at[j - 1],
                device_id=device(lax.rem(digit + j, size)),
                device_id_type=MESH,
            )
            copy.start()
            copies.append(copy)
        for copy in copies:
            copy.wait()
        begin = pl.multiple_of(begin - digit * count, PACK)
        count = count * size


def sum_devices(dp, frame, given):
    rows = given.shape[0]
    vmem = pl.BlockSpec(memory_space=pltpu.VMEM)
    scratch, sems, count = [pltpu.VMEM(given.shape, BF16)], [], rows
    for size in (lambda c, y, x, z: (c, x, y, z))(*factors(dp, frame)):
        count //= size
        slots = max(size - 1, 1)
        scratch.append(pltpu.VMEM((slots, count, LANES), BF16))
        sems += [pltpu.SemaphoreType.DMA((slots,))] * 4
    return pl.pallas_call(
        functools.partial(sum_kernel, dp, frame),
        out_shape=jax.ShapeDtypeStruct(given.shape, BF16),
        in_specs=[vmem],
        out_specs=vmem,
        scratch_shapes=scratch + sems,
        compiler_params=pltpu.CompilerParams(
            collective_id=1, has_side_effects=True, vmem_limit_bytes=32 * 2**20
        ),
        name="sum_devices",
    )(given)


def unpack_kernel(packed, g_in, g_gain, g_qkv, g_out, g_head):
    row = 0
    for ref in (g_in, g_qkv, g_out):
        height = ref.shape[0]
        for tile in range(ref.shape[1] // LANES):
            ref[:, tile * LANES : (tile + 1) * LANES] = packed[pl.ds(row, height), :].astype(F32)
            row += height
    for tile in range(g_head.shape[1] // LANES):
        small = packed[pl.ds(row, PACK), :].astype(F32)
        at = slice(tile * LANES, (tile + 1) * LANES)
        g_head[:, at] = small[0 : g_head.shape[0]]
        g_gain[:, at] = small[SUB : SUB + 1]
        row += PACK


def unpack(packed, shapes):
    vmem = pl.BlockSpec(memory_space=pltpu.VMEM)
    return pl.pallas_call(
        unpack_kernel,
        out_shape=[jax.ShapeDtypeStruct(shape, F32) for shape in shapes],
        in_specs=[vmem],
        out_specs=[vmem] * len(shapes),
        compiler_params=pltpu.CompilerParams(vmem_limit_bytes=32 * 2**20),
        name="unpack",
    )(packed)


def body(
    dp,
    frame,
    features,
    vis_block,
    vis_count,
    query_frame,
    query_block,
    query_cell,
    cotangent,
    w_in,
    gain,
    w_qkv,
    w_out,
    w_head,
):
    outs, trk_dev, frames = cotangent.shape[1:]
    hid = w_in.shape[1]
    ct = cotangent[0].reshape(outs, trk_dev // SUB, SUB, frames)
    ct = jnp.swapaxes(ct, 2, 3).reshape(outs, trk_dev * frames)
    ct = jnp.pad(ct, ((0, PACK - outs), (0, 0)))
    picked, patches = pick(features, vis_block, vis_count, query_frame, query_block, query_cell)
    corr = correlate(frame, picked, patches)
    rows = packed_rows((w_in.shape, w_qkv.shape, w_out.shape, (PACK, hid)), dp * frame)
    packed = layer(rows, corr, ct, w_in, gain.reshape(hid, 1), w_qkv, w_out, w_head)
    summed = sum_devices(dp, frame, packed)
    s_in, s_gain, s_qkv, s_out, s_head = unpack(
        summed, (w_in.shape, (1, hid), w_qkv.shape, w_out.shape, w_head.shape)
    )
    return (s_in, s_gain.reshape(hid), s_qkv, s_out, s_head)


def solution(mesh):
    in_specs = (
        P("dp", "frame", None, None, None),
        P("dp", None, "frame", None),
        P("dp", None, "frame"),
        P("dp", None),
        P("dp", None),
        P("dp", None),
        P("dp", None, "frame", None),
        P(),
        P(),
        P(),
        P(),
        P(),
    )
    out_specs = (P(), P(), P(), P(), P())
    run = functools.partial(body, mesh.shape["dp"], mesh.shape["frame"])
    return jax.shard_map(run, mesh=mesh, in_specs=in_specs, out_specs=out_specs, check_vma=False)
```

```python
import functools

import jax
import jax.numpy as jnp
from jax import lax
from jax.experimental import pallas as pl
from jax.experimental.pallas import tpu as pltpu
from jax.sharding import PartitionSpec as P

HEADS = 8
LANES = 128
SUB = 8
PACK = 16
CHUNKS = 4
MESH = pl.DeviceIdType.MESH
F32 = jnp.float32
BF16 = jnp.bfloat16


def dot_nn(left, right):
    return lax.dot_general(left, right, (((1,), (0,)), ((), ())), preferred_element_type=F32)


def dot_nt(left, right):
    return lax.dot_general(left, right, (((1,), (1,)), ((), ())), preferred_element_type=F32)


def dot_tn(left, right):
    return lax.dot_general(left, right, (((0,), (0,)), ((), ())), preferred_element_type=F32)


def pick_kernel(
    feats, vis_block, vis_count, q_frame, q_block, q_cell, queries, patches,
    s_block, s_count, s_frame, s_qblock, s_cell, tiles, picked, i_sem, p_sem, q_sem,
):
    fr_dev, cells, width = feats.shape[1], feats.shape[3], feats.shape[4]
    slots, groups = vis_block.shape[2], vis_block.shape[3]
    tracks = q_frame.shape[1]
    first = lax.axis_index("frame") * fr_dev
    loads = [
        pltpu.make_async_copy(src, dst, i_sem.at[i])
        for i, (src, dst) in enumerate(
            (
                (q_frame, s_frame),
                (q_block, s_qblock),
                (q_cell, s_cell),
                (vis_block, s_block),
                (vis_count, s_count),
            )
        )
    ]
    for load in loads:
        load.start()
    for load in loads[:3]:
        load.wait()

    @pl.loop(0, tracks // SUB)
    def _(step):
        for i in range(SUB):
            t = step * SUB + i
            local = jnp.clip(s_frame[0, t] - first, 0, fr_dev - 1)
            base = pl.multiple_of(lax.div(s_cell[0, t], PACK) * PACK, PACK)
            pltpu.make_async_copy(
                feats.at[0, local, s_qblock[0, t], pl.ds(base, PACK), :], tiles.at[t], q_sem
            ).start()

    for load in loads[3:]:
        load.wait()
    for g in range(groups):
        for f in range(fr_dev):
            for k in range(slots):
                pltpu.make_async_copy(
                    feats.at[0, f, s_block[0, f, k, g]],
                    patches.at[g, f, pl.ds(k * cells, cells)],
                    p_sem,
                ).start()

    row_id = lax.broadcasted_iota(jnp.int32, (PACK, width), 0)
    pltpu.make_async_copy(tiles, tiles, q_sem).wait()

    @pl.loop(0, tracks // SUB)
    def _(step):
        for i in range(SUB):
            t = step * SUB + i
            local = s_frame[0, t] - first
            inside = jnp.logical_and(local >= 0, local < fr_dev)
            row = jnp.where(inside, lax.rem(s_cell[0, t], PACK), PACK)
            kept = jnp.where(row_id == row, tiles[t].astype(F32), 0.0)
            picked[pl.ds(t, 1), :] = jnp.sum(kept, axis=0, keepdims=True)

    queries[...] = picked[...].astype(BF16)
    pltpu.make_async_copy(patches, patches, p_sem).wait()
    for g in range(groups):
        for f in range(fr_dev):
            for k in range(slots):

                @pl.when(k >= s_count[0, f, g])
                def _(g=g, f=f, k=k):
                    patches[g, f, k * cells : (k + 1) * cells] = jnp.zeros((cells, width), BF16)


def pick(feats, vis_block, vis_count, q_frame, q_block, q_cell):
    fr_dev, cells, width = feats.shape[1], feats.shape[3], feats.shape[4]
    groups, slots = vis_block.shape[1], vis_block.shape[3]
    tracks = q_frame.shape[1]
    vis_block = jnp.transpose(vis_block, (0, 2, 3, 1))
    vis_count = jnp.transpose(vis_count, (0, 2, 1))
    hbm = pl.BlockSpec(memory_space=pltpu.HBM)
    vmem = pl.BlockSpec(memory_space=pltpu.VMEM)
    arrays = (vis_block, vis_count, q_frame, q_block, q_cell)
    return pl.pallas_call(
        pick_kernel,
        out_shape=[
            jax.ShapeDtypeStruct((tracks, width), BF16),
            jax.ShapeDtypeStruct((groups, fr_dev, slots * cells, width), BF16),
        ],
        in_specs=[hbm] * 6,
        out_specs=[vmem, vmem],
        scratch_shapes=[pltpu.SMEM(array.shape, jnp.int32) for array in arrays]
        + [
            pltpu.VMEM((tracks, PACK, width), BF16),
            pltpu.VMEM((tracks, width), F32),
            pltpu.SemaphoreType.DMA((5,)),
            pltpu.SemaphoreType.DMA,
            pltpu.SemaphoreType.DMA,
        ],
        compiler_params=pltpu.CompilerParams(vmem_limit_bytes=60 * 2**20),
        name="pick",
    )(feats, *arrays)


def spread_cotangent(cot, tokens):
    outs, frames, tracks = cot.shape
    block = frames * SUB
    token = lax.broadcasted_iota(jnp.int32, (tracks, tokens), 1)
    track = lax.broadcasted_iota(jnp.int32, (tracks, tokens), 0)
    wanted = lax.div(token, block) * SUB + lax.rem(token, SUB)
    choose = jnp.where(track == wanted, 1.0, 0.0).astype(BF16)
    spread = dot_nn(cot[...].reshape(outs * frames, tracks), choose)
    token = lax.broadcasted_iota(jnp.int32, (frames, tokens), 1)
    row = lax.broadcasted_iota(jnp.int32, (frames, tokens), 0)
    here = lax.div(lax.rem(token, block), SUB) == row
    return [
        jnp.sum(
            jnp.where(here, spread[o * frames : (o + 1) * frames], 0.0), axis=0, keepdims=True
        )
        for o in range(outs)
    ]


def corr_kernel(
    n,
    picked, patches, cot, gain, w_in, w_qkv, w_out, w_head,
    out, w_in_t, w_qkv_t, w_out_t, ct, gain_col, d_y, datt_t,
    q_recv, c_send, head_pad, ct_pad, q_ssem, q_rsem, c_ssem, c_rsem,
):
    me = lax.axis_index("frame")
    groups, fr_dev, _, width = patches.shape
    in_group = picked.shape[0] // groups
    own = groups // n
    barrier = pltpu.get_barrier_semaphore()
    for j in range(1, n):
        pl.semaphore_signal(
            barrier, inc=1, device_id={"frame": lax.rem(me + j, n)}, device_id_type=MESH
        )
    w_in_t[...] = w_in[...].T
    w_out_t[...] = w_out[...].T
    pl.semaphore_wait(barrier, n - 1)
    copies = []
    for j in range(1, n):
        copy = pltpu.make_async_remote_copy(
            src_ref=picked,
            dst_ref=q_recv.at[j - 1],
            send_sem=q_ssem.at[j - 1],
            recv_sem=q_rsem.at[j - 1],
            device_id={"frame": lax.rem(me + j, n)},
            device_id_type=MESH,
        )
        copy.start()
        copies.append(copy)
    w_qkv_t[...] = w_qkv[...].T
    for copy in copies:
        copy.wait()
    total = picked[...].astype(F32)
    for j in range(1, n):
        total = total + q_recv[j - 1].astype(F32)
    query = total.astype(BF16)

    scale = width ** (-0.5)
    for g in range(groups):
        q_rows = query[g * in_group : (g + 1) * in_group]
        for f in range(fr_dev):
            corr = dot_nt(q_rows, patches[g, f]) * scale
            c_send[g // own, g % own, f] = corr.astype(BF16)
    copies = []
    for j in range(1, n):
        peer = lax.rem(me + j, n)
        copy = pltpu.make_async_remote_copy(
            src_ref=c_send.at[peer],
            dst_ref=out.at[me],
            send_sem=c_ssem.at[j - 1],
            recv_sem=c_rsem.at[j - 1],
            device_id={"frame": peer},
            device_id_type=MESH,
        )
        copy.start()
        copies.append(copy)
    out[me] = c_send[me]

    head_pad[...] = jnp.zeros_like(head_pad)
    head_pad[0 : w_head.shape[0], :] = w_head[...].astype(F32)
    ct_pad[...] = jnp.zeros_like(ct_pad)
    for o, row in enumerate(spread_cotangent(cot, ct_pad.shape[1])):
        ct_pad[o : o + 1, :] = row
    ct_rows = ct_pad[...].astype(BF16)
    ct[...] = ct_rows
    dy = dot_tn(head_pad[...].astype(BF16), ct_rows)
    d_y[...] = dy
    datt_t[...] = dot_nn(w_out[...], dy.astype(BF16)).astype(BF16)
    gain_col[...] = jnp.broadcast_to(gain[...], (LANES, gain.shape[1])).T[:, 0:1]
    for copy in copies:
        copy.wait()


def correlate(n, picked, patches, cot, gain, w_in, w_qkv, w_out, w_head):
    groups, fr_dev, cells, _ = patches.shape
    tracks, width = picked.shape
    hid = w_in.shape[1]
    tokens = cot.shape[1] * cot.shape[2]
    shape = (n, groups // n, fr_dev, tracks // groups, cells)
    vmem = pl.BlockSpec(memory_space=pltpu.VMEM)
    sems = pltpu.SemaphoreType.DMA((n - 1,))
    outs = [
        (shape, BF16),
        (w_in.shape[::-1], BF16),
        (w_qkv.shape[::-1], BF16),
        (w_out.shape[::-1], BF16),
        ((PACK, tokens), BF16),
        ((hid, 1), F32),
        ((hid, tokens), F32),
        ((hid, tokens), BF16),
    ]
    return pl.pallas_call(
        functools.partial(corr_kernel, n),
        out_shape=[jax.ShapeDtypeStruct(*item) for item in outs],
        in_specs=[vmem] * 8,
        out_specs=[vmem] * len(outs),
        scratch_shapes=[
            pltpu.VMEM((n - 1, tracks, width), BF16),
            pltpu.VMEM(shape, BF16),
            pltpu.VMEM((PACK, hid), F32),
            pltpu.VMEM((PACK, tokens), F32),
            sems,
            sems,
            sems,
            sems,
        ],
        compiler_params=pltpu.CompilerParams(
            collective_id=0, has_side_effects=True, vmem_limit_bytes=32 * 2**20
        ),
        name="correlate",
    )(picked, patches, cot, gain, w_in, w_qkv, w_out, w_head)


def layer_kernel(
    corr, w_in_t, w_qkv_t, w_out_t, ct, gain, dy_ref, datt_t, w_qkv, packed, qkv_t, dqkv_t, att_t
):
    n, own, fr_dev, in_group, width = corr.shape
    frames = n * fr_dev
    hid = w_in_t.shape[0]
    size = hid // HEADS
    block = frames * SUB
    halves = in_group // SUB
    tokens = own * halves * block

    c32 = corr[...].astype(F32)
    parts = []
    for g in range(own):
        piece = c32[:, g].reshape(frames, halves, SUB, width)
        for half in range(halves):
            parts.append(piece[:, half].reshape(block, width))
    rows32 = jnp.concatenate(parts, axis=0)
    rows = rows32.astype(BF16)
    rows_t = rows32.T.astype(BF16)

    x_zero = dot_nn(w_in_t[...], rows_t)
    centred = x_zero - jnp.mean(x_zero, axis=0, keepdims=True)
    inv_std = lax.rsqrt(jnp.mean(centred * centred, axis=0, keepdims=True) + 1e-05)
    normed = centred * inv_std
    gain_col = gain[...]
    hidden = (normed * gain_col).astype(BF16)
    qkv_t[...] = dot_nn(w_qkv_t[...], hidden).astype(BF16)

    ct_rows = ct[...]
    d_y = dy_ref[...]
    d_y16 = d_y.astype(BF16)

    scale = size ** (-0.5)
    key_id = lax.broadcasted_iota(jnp.int32, (block, block), 0)
    query_id = lax.broadcasted_iota(jnp.int32, (block, block), 1)
    same = lax.rem(key_id, SUB) == lax.rem(query_id, SUB)
    to_exp2 = scale * 1.4426950408889634

    for b in range(tokens // block):
        at = pl.ds(b * block, block)
        for head in range(HEADS):
            mine = pl.ds(head * size, size)
            q = qkv_t[mine, at]
            k = qkv_t[pl.ds(hid + head * size, size), at]
            v = qkv_t[pl.ds(2 * hid + head * size, size), at]
            d_att = datt_t[mine, at]
            scores = jnp.where(same, dot_tn(k, q), -1e30)
            top = jnp.max(scores, axis=0, keepdims=True)
            powers = jnp.exp2((scores - top) * to_exp2)
            probs = powers * (1.0 / jnp.sum(powers, axis=0, keepdims=True))
            probs16 = probs.astype(BF16)
            att_t[mine, at] = dot_nn(v, probs16).astype(BF16)
            d_v = dot_nt(d_att, probs16)
            d_probs = dot_tn(v, d_att).astype(BF16).astype(F32)
            weighted = probs * d_probs
            d_scores = weighted - probs * jnp.sum(weighted, axis=0, keepdims=True)
            d_scores = d_scores.astype(BF16)
            d_q = dot_nn(k, d_scores) * scale
            d_k = dot_nt(q, d_scores) * scale
            dqkv_t[mine, at] = d_q.astype(BF16)
            dqkv_t[pl.ds(hid + head * size, size), at] = d_k.astype(BF16)
            dqkv_t[pl.ds(2 * hid + head * size, size), at] = d_v.astype(BF16)

    def put(row, value):
        for tile in range(value.shape[1] // LANES):
            packed[pl.ds(row, value.shape[0]), :] = value[
                :, tile * LANES : (tile + 1) * LANES
            ].astype(BF16)
            row += value.shape[0]
        return row

    att = att_t[...]
    y_out = (x_zero + dot_nn(w_out_t[...], att)).astype(BF16)
    d_qkv = dqkv_t[...]
    d_hidden = dot_nn(w_qkv[...], d_qkv)
    product = d_hidden * normed
    d_norm = d_hidden * gain_col
    d_x = (
        inv_std
        * (
            d_norm
            - jnp.mean(d_norm, axis=0, keepdims=True)
            - normed * jnp.mean(d_norm * normed, axis=0, keepdims=True)
        )
        + d_y
    )
    row = put(0, dot_nt(rows_t, d_x.astype(BF16)))
    row = put(row, dot_nt(hidden, d_qkv))
    row = put(row, dot_nt(att, d_y16))
    high = product.astype(BF16)
    low = (product - high.astype(F32)).astype(BF16)
    picks = (lax.broadcasted_iota(jnp.int32, (PACK, tokens), 0) == SUB).astype(F32).astype(BF16)
    row = put(row, dot_nt(ct_rows, y_out) + dot_nt(picks, high) + dot_nt(picks, low))
    if row < packed.shape[0]:
        packed[pl.ds(row, packed.shape[0] - row), :] = jnp.zeros(
            (packed.shape[0] - row, LANES), BF16
        )


def packed_rows(shapes, devices):
    rows = sum(-(-r // PACK) * PACK * (c // LANES) for r, c in shapes)
    step = PACK * devices
    return -(-rows // step) * step


def layer(rows, prepared, w_qkv):
    hid, tokens = prepared[-1].shape
    vmem = pl.BlockSpec(memory_space=pltpu.VMEM)
    return pl.pallas_call(
        layer_kernel,
        out_shape=jax.ShapeDtypeStruct((rows, LANES), BF16),
        in_specs=[vmem] * 9,
        out_specs=vmem,
        scratch_shapes=[
            pltpu.VMEM((3 * hid, tokens), BF16),
            pltpu.VMEM((3 * hid, tokens), BF16),
            pltpu.VMEM((hid, tokens), BF16),
        ],
        compiler_params=pltpu.CompilerParams(vmem_limit_bytes=48 * 2**20),
        name="layer",
    )(*prepared, w_qkv)


def factors(dp, frame):
    core = 2 if frame % 2 == 0 else 1
    mid = frame // core
    low = mid if dp % mid == 0 else 1
    return core, mid, low, dp // low


def stages(dp, frame):
    n_core, n_y, n_x, n_z = factors(dp, frame)
    me_d, me_f = lax.axis_index("dp"), lax.axis_index("frame")
    core, y = lax.rem(me_f, n_core), lax.div(me_f, n_core)
    x, z = lax.rem(me_d, n_x), lax.div(me_d, n_x)
    swap = core if n_core == 2 and n_x == n_y else 0

    def device(core_at, y_at, x_at, z_at):
        return (z_at * n_x + x_at, y_at * n_core + core_at)

    keep = 1 - swap
    return (
        (n_core, core, lambda d: device(d, y, x, z)),
        (n_x, keep * x + swap * y, lambda d: device(core, keep * y + swap * d, keep * d + swap * x, z)),
        (n_y, keep * y + swap * x, lambda d: device(core, keep * d + swap * y, keep * x + swap * d, z)),
        (n_z, z, lambda d: device(core, y, x, d)),
    )


def chunk_bounds(rows, devices):
    units = rows // (PACK * devices)
    chunks = min(CHUNKS, units)
    sizes = [(units + chunks - 1 - c) // chunks * PACK * devices for c in range(chunks)]
    return [(sum(sizes[:c]), sizes[c]) for c in range(chunks)]


def sum_kernel(dp, frame, given, out, work, r0, r1, r2, r3, rs_send, rs_recv, ag_send, ag_recv):
    plan = stages(dp, frame)
    last = len(plan) - 1
    recvs = (r0, r1, r2, r3)
    bounds = chunk_bounds(given.shape[0], dp * frame)
    barrier = pltpu.get_barrier_semaphore()
    peers = 0
    for size, digit, device in plan:
        for j in range(1, size):
            pl.semaphore_signal(
                barrier, inc=1, device_id=device(lax.rem(digit + j, size)), device_id_type=MESH
            )
            peers += 1
    pl.semaphore_wait(barrier, peers)

    begins = [begin for begin, _ in bounds]
    counts = [count for _, count in bounds]
    offsets = [begin for begin, _ in bounds]
    flying = [[] for _ in bounds]

    def scatter_start(c, at):
        size, digit, device = plan[at]
        source = given if at == 0 else work
        part = counts[c] // size
        offsets[c] //= size
        for j in range(1, size):
            peer = lax.rem(digit + j, size)
            copy = pltpu.make_async_remote_copy(
                src_ref=source.at[pl.ds(pl.multiple_of(begins[c] + peer * part, PACK), part)],
                dst_ref=recvs[at].at[j - 1, pl.ds(offsets[c], part)],
                send_sem=rs_send.at[c, at, j - 1],
                recv_sem=rs_recv.at[c, at, j - 1],
                device_id=device(peer),
                device_id_type=MESH,
            )
            copy.start()
            flying[c].append(copy)

    def scatter_end(c, at):
        size, digit, device = plan[at]
        source = given if at == 0 else work
        target = out if at == last else work
        part = counts[c] // size
        for copy in flying[c]:
            copy.wait()
        flying[c] = []
        begins[c] = pl.multiple_of(begins[c] + digit * part, PACK)
        counts[c] = part
        total = source[pl.ds(begins[c], part), :].astype(F32)
        for j in range(1, size):
            total = total + recvs[at][j - 1, pl.ds(offsets[c], part), :].astype(F32)
        target[pl.ds(begins[c], part), :] = total.astype(BF16)

    def gather_start(c, at):
        size, digit, device = plan[at]
        for j in range(1, size):
            here = out.at[pl.ds(begins[c], counts[c])]
            copy = pltpu.make_async_remote_copy(
                src_ref=here,
                dst_ref=here,
                send_sem=ag_send.at[c, at, j - 1],
                recv_sem=ag_recv.at[c, at, j - 1],
                device_id=device(lax.rem(digit + j, size)),
                device_id_type=MESH,
            )
            copy.start()
            flying[c].append(copy)

    def gather_end(c, at):
        size, digit, device = plan[at]
        for copy in flying[c]:
            copy.wait()
        flying[c] = []
        begins[c] = pl.multiple_of(begins[c] - digit * counts[c], PACK)
        counts[c] = counts[c] * size

    steps = [(scatter_start, scatter_end, at) for at in range(last + 1)]
    steps += [(gather_start, gather_end, at) for at in range(last, -1, -1)]
    for tick in range(len(steps) + len(bounds)):
        for c in range(len(bounds)):
            step = tick - c
            if 1 <= step <= len(steps):
                steps[step - 1][1](c, steps[step - 1][2])
            if 0 <= step < len(steps):
                steps[step][0](c, steps[step][2])


def sum_devices(dp, frame, given):
    rows = given.shape[0]
    n_core, n_y, n_x, n_z = factors(dp, frame)
    sizes = (n_core, n_x, n_y, n_z)
    vmem = pl.BlockSpec(memory_space=pltpu.VMEM)
    scratch, count = [pltpu.VMEM(given.shape, BF16)], rows
    for size in sizes:
        count //= size
        scratch.append(pltpu.VMEM((max(size - 1, 1), count, LANES), BF16))
    chunks = len(chunk_bounds(rows, dp * frame))
    sems = pltpu.SemaphoreType.DMA((chunks, len(sizes), max(max(sizes) - 1, 1)))
    return pl.pallas_call(
        functools.partial(sum_kernel, dp, frame),
        out_shape=jax.ShapeDtypeStruct(given.shape, BF16),
        in_specs=[vmem],
        out_specs=vmem,
        scratch_shapes=scratch + [sems] * 4,
        compiler_params=pltpu.CompilerParams(
            collective_id=1, has_side_effects=True, vmem_limit_bytes=32 * 2**20
        ),
        name="sum_devices",
    )(given)


def unpack_kernel(packed, g_in, g_gain, g_qkv, g_out, g_head):
    row = 0
    for ref in (g_in, g_qkv, g_out):
        height = ref.shape[0]
        for tile in range(ref.shape[1] // LANES):
            ref[:, tile * LANES : (tile + 1) * LANES] = packed[pl.ds(row, height), :].astype(F32)
            row += height
    for tile in range(g_head.shape[1] // LANES):
        small = packed[pl.ds(row, PACK), :].astype(F32)
        at = slice(tile * LANES, (tile + 1) * LANES)
        g_head[:, at] = small[0 : g_head.shape[0]]
        g_gain[at] = small[SUB]
        row += PACK


def unpack(packed, shapes):
    vmem = pl.BlockSpec(memory_space=pltpu.VMEM)
    return pl.pallas_call(
        unpack_kernel,
        out_shape=[jax.ShapeDtypeStruct(shape, F32) for shape in shapes],
        in_specs=[vmem],
        out_specs=[vmem] * len(shapes),
        compiler_params=pltpu.CompilerParams(vmem_limit_bytes=32 * 2**20),
        name="unpack",
    )(packed)


def body(
    dp,
    frame,
    features,
    vis_block,
    vis_count,
    query_frame,
    query_block,
    query_cell,
    cotangent,
    w_in,
    gain,
    w_qkv,
    w_out,
    w_head,
):
    hid = w_in.shape[1]
    cot = jnp.swapaxes(cotangent[0], 1, 2)
    picked, patches = pick(features, vis_block, vis_count, query_frame, query_block, query_cell)
    prepared = correlate(
        frame, picked, patches, cot, gain.reshape(1, hid), w_in, w_qkv, w_out, w_head
    )
    rows = packed_rows((w_in.shape, w_qkv.shape, w_out.shape, (PACK, hid)), dp * frame)
    packed = layer(rows, prepared, w_qkv)
    summed = sum_devices(dp, frame, packed)
    return tuple(unpack(summed, (w_in.shape, gain.shape, w_qkv.shape, w_out.shape, w_head.shape)))


def solution(mesh):
    in_specs = (
        P("dp", "frame", None, None, None),
        P("dp", None, "frame", None),
        P("dp", None, "frame"),
        P("dp", None),
        P("dp", None),
        P("dp", None),
        P("dp", None, "frame", None),
        P(),
        P(),
        P(),
        P(),
        P(),
    )
    out_specs = (P(), P(), P(), P(), P())
    run = functools.partial(body, mesh.shape["dp"], mesh.shape["frame"])
    return jax.shard_map(run, mesh=mesh, in_specs=in_specs, out_specs=out_specs, check_vma=False)
```

```python
import functools

import jax
import jax.numpy as jnp
from jax import lax
from jax.experimental import pallas as pl
from jax.experimental.pallas import tpu as pltpu
from jax.sharding import PartitionSpec as P

HEADS = 8
LANES = 128
SUB = 8
PACK = 16
CHUNKS = 3
MESH = pl.DeviceIdType.MESH
F32 = jnp.float32
BF16 = jnp.bfloat16


def dot_nn(left, right):
    return lax.dot_general(left, right, (((1,), (0,)), ((), ())), preferred_element_type=F32)


def dot_nt(left, right):
    return lax.dot_general(left, right, (((1,), (1,)), ((), ())), preferred_element_type=F32)


def dot_tn(left, right):
    return lax.dot_general(left, right, (((0,), (0,)), ((), ())), preferred_element_type=F32)


def pick_kernel(
    feats, vis_block, vis_count, q_frame, q_block, q_cell, queries, patches,
    s_block, s_count, s_frame, s_qblock, s_cell, tiles, picked, i_sem, p_sem, q_sem,
):
    fr_dev, cells, width = feats.shape[1], feats.shape[3], feats.shape[4]
    slots, groups = vis_block.shape[2], vis_block.shape[3]
    tracks = q_frame.shape[1]
    first = lax.axis_index("frame") * fr_dev
    loads = [
        pltpu.make_async_copy(src, dst, i_sem.at[i])
        for i, (src, dst) in enumerate(
            (
                (q_frame, s_frame),
                (q_block, s_qblock),
                (q_cell, s_cell),
                (vis_block, s_block),
                (vis_count, s_count),
            )
        )
    ]
    for load in loads:
        load.start()
    for load in loads[:3]:
        load.wait()

    @pl.loop(0, tracks // SUB)
    def _(step):
        for i in range(SUB):
            t = step * SUB + i
            local = jnp.clip(s_frame[0, t] - first, 0, fr_dev - 1)
            base = pl.multiple_of(lax.div(s_cell[0, t], PACK) * PACK, PACK)
            pltpu.make_async_copy(
                feats.at[0, local, s_qblock[0, t], pl.ds(base, PACK), :], tiles.at[t], q_sem
            ).start()

    for load in loads[3:]:
        load.wait()
    for g in range(groups):
        for f in range(fr_dev):
            for k in range(slots):
                pltpu.make_async_copy(
                    feats.at[0, f, s_block[0, f, k, g]],
                    patches.at[g, f, pl.ds(k * cells, cells)],
                    p_sem,
                ).start()

    row_id = lax.broadcasted_iota(jnp.int32, (PACK, width), 0)
    pltpu.make_async_copy(tiles, tiles, q_sem).wait()

    @pl.loop(0, tracks // SUB)
    def _(step):
        for i in range(SUB):
            t = step * SUB + i
            local = s_frame[0, t] - first
            inside = jnp.logical_and(local >= 0, local < fr_dev)
            row = jnp.where(inside, lax.rem(s_cell[0, t], PACK), PACK)
            kept = jnp.where(row_id == row, tiles[t].astype(F32), 0.0)
            picked[pl.ds(t, 1), :] = jnp.sum(kept, axis=0, keepdims=True)

    queries[...] = picked[...].astype(BF16)
    pltpu.make_async_copy(patches, patches, p_sem).wait()
    for g in range(groups):
        for f in range(fr_dev):
            for k in range(slots):

                @pl.when(k >= s_count[0, f, g])
                def _(g=g, f=f, k=k):
                    patches[g, f, k * cells : (k + 1) * cells] = jnp.zeros((cells, width), BF16)


def pick(feats, vis_block, vis_count, q_frame, q_block, q_cell):
    fr_dev, cells, width = feats.shape[1], feats.shape[3], feats.shape[4]
    groups, slots = vis_block.shape[1], vis_block.shape[3]
    tracks = q_frame.shape[1]
    vis_block = jnp.transpose(vis_block, (0, 2, 3, 1))
    vis_count = jnp.transpose(vis_count, (0, 2, 1))
    hbm = pl.BlockSpec(memory_space=pltpu.HBM)
    vmem = pl.BlockSpec(memory_space=pltpu.VMEM)
    arrays = (vis_block, vis_count, q_frame, q_block, q_cell)
    return pl.pallas_call(
        pick_kernel,
        out_shape=[
            jax.ShapeDtypeStruct((tracks, width), BF16),
            jax.ShapeDtypeStruct((groups, fr_dev, slots * cells, width), BF16),
        ],
        in_specs=[hbm] * 6,
        out_specs=[vmem, vmem],
        scratch_shapes=[pltpu.SMEM(array.shape, jnp.int32) for array in arrays]
        + [
            pltpu.VMEM((tracks, PACK, width), BF16),
            pltpu.VMEM((tracks, width), F32),
            pltpu.SemaphoreType.DMA((5,)),
            pltpu.SemaphoreType.DMA,
            pltpu.SemaphoreType.DMA,
        ],
        compiler_params=pltpu.CompilerParams(vmem_limit_bytes=60 * 2**20),
        name="pick",
    )(feats, *arrays)


def spread_cotangent(cot, tokens):
    outs, frames, tracks = cot.shape
    block = frames * SUB
    token = lax.broadcasted_iota(jnp.int32, (tracks, tokens), 1)
    track = lax.broadcasted_iota(jnp.int32, (tracks, tokens), 0)
    wanted = lax.div(token, block) * SUB + lax.rem(token, SUB)
    choose = jnp.where(track == wanted, 1.0, 0.0).astype(BF16)
    spread = dot_nn(cot[...].reshape(outs * frames, tracks), choose)
    token = lax.broadcasted_iota(jnp.int32, (frames, tokens), 1)
    row = lax.broadcasted_iota(jnp.int32, (frames, tokens), 0)
    here = lax.div(lax.rem(token, block), SUB) == row
    return [
        jnp.sum(
            jnp.where(here, spread[o * frames : (o + 1) * frames], 0.0), axis=0, keepdims=True
        )
        for o in range(outs)
    ]


def corr_kernel(
    n,
    picked, patches, cot, gain, w_in, w_qkv, w_out, w_head,
    out, w_in_t, w_qkv_t, w_out_t, ct, gain_col, d_y, datt_t,
    q_recv, c_send, head_pad, ct_pad, q_ssem, q_rsem, c_ssem, c_rsem,
):
    me = lax.axis_index("frame")
    groups, fr_dev, _, width = patches.shape
    in_group = picked.shape[0] // groups
    own = groups // n
    barrier = pltpu.get_barrier_semaphore()
    for j in range(1, n):
        pl.semaphore_signal(
            barrier, inc=1, device_id={"frame": lax.rem(me + j, n)}, device_id_type=MESH
        )
    w_in_t[...] = w_in[...].T
    w_out_t[...] = w_out[...].T
    pl.semaphore_wait(barrier, n - 1)
    copies = []
    for j in range(1, n):
        copy = pltpu.make_async_remote_copy(
            src_ref=picked,
            dst_ref=q_recv.at[j - 1],
            send_sem=q_ssem.at[j - 1],
            recv_sem=q_rsem.at[j - 1],
            device_id={"frame": lax.rem(me + j, n)},
            device_id_type=MESH,
        )
        copy.start()
        copies.append(copy)
    w_qkv_t[...] = w_qkv[...].T
    for copy in copies:
        copy.wait()
    total = picked[...].astype(F32)
    for j in range(1, n):
        total = total + q_recv[j - 1].astype(F32)
    query = total.astype(BF16)

    scale = width ** (-0.5)
    for g in range(groups):
        q_rows = query[g * in_group : (g + 1) * in_group]
        for f in range(fr_dev):
            corr = dot_nt(q_rows, patches[g, f]) * scale
            c_send[g // own, g % own, f] = corr.astype(BF16)
    copies = []
    for j in range(1, n):
        peer = lax.rem(me + j, n)
        copy = pltpu.make_async_remote_copy(
            src_ref=c_send.at[peer],
            dst_ref=out.at[me],
            send_sem=c_ssem.at[j - 1],
            recv_sem=c_rsem.at[j - 1],
            device_id={"frame": peer},
            device_id_type=MESH,
        )
        copy.start()
        copies.append(copy)
    out[me] = c_send[me]

    head_pad[...] = jnp.zeros_like(head_pad)
    head_pad[0 : w_head.shape[0], :] = w_head[...].astype(F32)
    ct_pad[...] = jnp.zeros_like(ct_pad)
    for o, row in enumerate(spread_cotangent(cot, ct_pad.shape[1])):
        ct_pad[o : o + 1, :] = row
    ct_rows = ct_pad[...].astype(BF16)
    ct[...] = ct_rows
    dy = dot_tn(head_pad[...].astype(BF16), ct_rows)
    d_y[...] = dy
    datt_t[...] = dot_nn(w_out[...], dy.astype(BF16)).astype(BF16)
    gain_col[...] = jnp.broadcast_to(gain[...], (LANES, gain.shape[1])).T[:, 0:1]
    for copy in copies:
        copy.wait()


def correlate(n, picked, patches, cot, gain, w_in, w_qkv, w_out, w_head):
    groups, fr_dev, cells, _ = patches.shape
    tracks, width = picked.shape
    hid = w_in.shape[1]
    tokens = cot.shape[1] * cot.shape[2]
    shape = (n, groups // n, fr_dev, tracks // groups, cells)
    vmem = pl.BlockSpec(memory_space=pltpu.VMEM)
    sems = pltpu.SemaphoreType.DMA((n - 1,))
    outs = [
        (shape, BF16),
        (w_in.shape[::-1], BF16),
        (w_qkv.shape[::-1], BF16),
        (w_out.shape[::-1], BF16),
        ((PACK, tokens), BF16),
        ((hid, 1), F32),
        ((hid, tokens), F32),
        ((hid, tokens), BF16),
    ]
    return pl.pallas_call(
        functools.partial(corr_kernel, n),
        out_shape=[jax.ShapeDtypeStruct(*item) for item in outs],
        in_specs=[vmem] * 8,
        out_specs=[vmem] * len(outs),
        scratch_shapes=[
            pltpu.VMEM((n - 1, tracks, width), BF16),
            pltpu.VMEM(shape, BF16),
            pltpu.VMEM((PACK, hid), F32),
            pltpu.VMEM((PACK, tokens), F32),
            sems,
            sems,
            sems,
            sems,
        ],
        compiler_params=pltpu.CompilerParams(
            collective_id=0, has_side_effects=True, vmem_limit_bytes=32 * 2**20
        ),
        name="correlate",
    )(picked, patches, cot, gain, w_in, w_qkv, w_out, w_head)


def layer_kernel(
    corr, w_in_t, w_qkv_t, w_out_t, ct, gain, dy_ref, datt_t, w_qkv, packed, qkv_t, dqkv_t, att_t
):
    n, own, fr_dev, in_group, width = corr.shape
    frames = n * fr_dev
    hid = w_in_t.shape[0]
    size = hid // HEADS
    block = frames * SUB
    halves = in_group // SUB
    tokens = own * halves * block

    c32 = corr[...].astype(F32)
    parts = []
    for g in range(own):
        piece = c32[:, g].reshape(frames, halves, SUB, width)
        for half in range(halves):
            parts.append(piece[:, half].reshape(block, width))
    rows32 = jnp.concatenate(parts, axis=0)
    rows = rows32.astype(BF16)
    rows_t = rows32.T.astype(BF16)

    x_zero = dot_nn(w_in_t[...], rows_t)
    centred = x_zero - jnp.mean(x_zero, axis=0, keepdims=True)
    inv_std = lax.rsqrt(jnp.mean(centred * centred, axis=0, keepdims=True) + 1e-05)
    normed = centred * inv_std
    gain_col = gain[...]
    hidden = (normed * gain_col).astype(BF16)
    qkv_t[...] = dot_nn(w_qkv_t[...], hidden).astype(BF16)

    ct_rows = ct[...]
    d_y = dy_ref[...]
    d_y16 = d_y.astype(BF16)

    scale = size ** (-0.5)
    key_id = lax.broadcasted_iota(jnp.int32, (block, block), 0)
    query_id = lax.broadcasted_iota(jnp.int32, (block, block), 1)
    same = lax.rem(key_id, SUB) == lax.rem(query_id, SUB)
    to_exp2 = scale * 1.4426950408889634

    for b in range(tokens // block):
        at = pl.ds(b * block, block)
        for head in range(HEADS):
            mine = pl.ds(head * size, size)
            q = qkv_t[mine, at]
            k = qkv_t[pl.ds(hid + head * size, size), at]
            v = qkv_t[pl.ds(2 * hid + head * size, size), at]
            d_att = datt_t[mine, at]
            scores = jnp.where(same, dot_tn(k, q), -1e30)
            top = jnp.max(scores, axis=0, keepdims=True)
            powers = jnp.exp2((scores - top) * to_exp2)
            probs = powers * (1.0 / jnp.sum(powers, axis=0, keepdims=True))
            probs16 = probs.astype(BF16)
            att_t[mine, at] = dot_nn(v, probs16).astype(BF16)
            d_v = dot_nt(d_att, probs16)
            d_probs = dot_tn(v, d_att).astype(BF16).astype(F32)
            weighted = probs * d_probs
            d_scores = weighted - probs * jnp.sum(weighted, axis=0, keepdims=True)
            d_scores = d_scores.astype(BF16)
            d_q = dot_nn(k, d_scores) * scale
            d_k = dot_nt(q, d_scores) * scale
            dqkv_t[mine, at] = d_q.astype(BF16)
            dqkv_t[pl.ds(hid + head * size, size), at] = d_k.astype(BF16)
            dqkv_t[pl.ds(2 * hid + head * size, size), at] = d_v.astype(BF16)

    def put(row, value):
        for tile in range(value.shape[1] // LANES):
            packed[pl.ds(row, value.shape[0]), :] = value[
                :, tile * LANES : (tile + 1) * LANES
            ].astype(BF16)
            row += value.shape[0]
        return row

    att = att_t[...]
    y_out = (x_zero + dot_nn(w_out_t[...], att)).astype(BF16)
    d_qkv = dqkv_t[...]
    d_hidden = dot_nn(w_qkv[...], d_qkv)
    product = d_hidden * normed
    d_norm = d_hidden * gain_col
    d_x = (
        inv_std
        * (
            d_norm
            - jnp.mean(d_norm, axis=0, keepdims=True)
            - normed * jnp.mean(d_norm * normed, axis=0, keepdims=True)
        )
        + d_y
    )
    row = put(0, dot_nt(rows_t, d_x.astype(BF16)))
    row = put(row, dot_nt(hidden, d_qkv))
    row = put(row, dot_nt(att, d_y16))
    high = product.astype(BF16)
    low = (product - high.astype(F32)).astype(BF16)
    picks = (lax.broadcasted_iota(jnp.int32, (PACK, tokens), 0) == SUB).astype(F32).astype(BF16)
    row = put(row, dot_nt(ct_rows, y_out) + dot_nt(picks, high) + dot_nt(picks, low))
    if row < packed.shape[0]:
        packed[pl.ds(row, packed.shape[0] - row), :] = jnp.zeros(
            (packed.shape[0] - row, LANES), BF16
        )


def packed_rows(shapes, devices):
    rows = sum(-(-r // PACK) * PACK * (c // LANES) for r, c in shapes)
    step = PACK * devices
    return -(-rows // step) * step


def layer(rows, prepared, w_qkv):
    hid, tokens = prepared[-1].shape
    vmem = pl.BlockSpec(memory_space=pltpu.VMEM)
    return pl.pallas_call(
        layer_kernel,
        out_shape=jax.ShapeDtypeStruct((rows, LANES), BF16),
        in_specs=[vmem] * 9,
        out_specs=vmem,
        scratch_shapes=[
            pltpu.VMEM((3 * hid, tokens), BF16),
            pltpu.VMEM((3 * hid, tokens), BF16),
            pltpu.VMEM((hid, tokens), BF16),
        ],
        compiler_params=pltpu.CompilerParams(vmem_limit_bytes=48 * 2**20),
        name="layer",
    )(*prepared, w_qkv)


def factors(dp, frame):
    core = 2 if frame % 2 == 0 else 1
    mid = frame // core
    low = mid if dp % mid == 0 else 1
    return core, mid, low, dp // low


def stages(dp, frame):
    n_core, n_y, n_x, n_z = factors(dp, frame)
    me_d, me_f = lax.axis_index("dp"), lax.axis_index("frame")
    core, y = lax.rem(me_f, n_core), lax.div(me_f, n_core)
    x, z = lax.rem(me_d, n_x), lax.div(me_d, n_x)
    swap = core if n_core == 2 and n_x == n_y else 0

    def device(core_at, y_at, x_at, z_at):
        return (z_at * n_x + x_at, y_at * n_core + core_at)

    return (
        (n_core, core, lambda d: device(d, y, x, z)),
        (n_x * n_y, y * n_x + x, lambda d: device(core, lax.div(d, n_x), lax.rem(d, n_x), z)),
        (n_z, z, lambda d: device(core, y, x, d)),
    )


def chunk_bounds(rows, devices):
    units = rows // (PACK * devices)
    chunks = min(CHUNKS, units)
    sizes = [(units + chunks - 1 - c) // chunks * PACK * devices for c in range(chunks)]
    return [(sum(sizes[:c]), sizes[c]) for c in range(chunks)]


def sum_kernel(dp, frame, given, out, work, r0, r1, r2, rs_send, rs_recv, ag_send, ag_recv):
    plan = stages(dp, frame)
    last = len(plan) - 1
    recvs = (r0, r1, r2)
    bounds = chunk_bounds(given.shape[0], dp * frame)
    barrier = pltpu.get_barrier_semaphore()
    peers = 0
    for size, digit, device in plan:
        for j in range(1, size):
            pl.semaphore_signal(
                barrier, inc=1, device_id=device(lax.rem(digit + j, size)), device_id_type=MESH
            )
            peers += 1
    pl.semaphore_wait(barrier, peers)

    begins = [begin for begin, _ in bounds]
    counts = [count for _, count in bounds]
    offsets = [begin for begin, _ in bounds]
    flying = [[] for _ in bounds]

    def scatter_start(c, at):
        size, digit, device = plan[at]
        source = given if at == 0 else work
        part = counts[c] // size
        offsets[c] //= size
        for j in range(1, size):
            peer = lax.rem(digit + j, size)
            copy = pltpu.make_async_remote_copy(
                src_ref=source.at[pl.ds(pl.multiple_of(begins[c] + peer * part, PACK), part)],
                dst_ref=recvs[at].at[j - 1, pl.ds(offsets[c], part)],
                send_sem=rs_send.at[c, at, j - 1],
                recv_sem=rs_recv.at[c, at, j - 1],
                device_id=device(peer),
                device_id_type=MESH,
            )
            copy.start()
            flying[c].append(copy)

    def scatter_end(c, at):
        size, digit, device = plan[at]
        source = given if at == 0 else work
        target = out if at == last else work
        part = counts[c] // size
        for copy in flying[c]:
            copy.wait()
        flying[c] = []
        begins[c] = pl.multiple_of(begins[c] + digit * part, PACK)
        counts[c] = part
        total = source[pl.ds(begins[c], part), :].astype(F32)
        for j in range(1, size):
            total = total + recvs[at][j - 1, pl.ds(offsets[c], part), :].astype(F32)
        target[pl.ds(begins[c], part), :] = total.astype(BF16)

    def gather_start(c, at):
        size, digit, device = plan[at]
        for j in range(1, size):
            here = out.at[pl.ds(begins[c], counts[c])]
            copy = pltpu.make_async_remote_copy(
                src_ref=here,
                dst_ref=here,
                send_sem=ag_send.at[c, at, j - 1],
                recv_sem=ag_recv.at[c, at, j - 1],
                device_id=device(lax.rem(digit + j, size)),
                device_id_type=MESH,
            )
            copy.start()
            flying[c].append(copy)

    def gather_end(c, at):
        size, digit, device = plan[at]
        for copy in flying[c]:
            copy.wait()
        flying[c] = []
        begins[c] = pl.multiple_of(begins[c] - digit * counts[c], PACK)
        counts[c] = counts[c] * size

    steps = [(scatter_start, scatter_end, at) for at in range(last + 1)]
    steps += [(gather_start, gather_end, at) for at in range(last, -1, -1)]
    for step in range(len(steps) + 1):
        for c in range(len(bounds)):
            if step > 0:
                steps[step - 1][1](c, steps[step - 1][2])
            if step < len(steps):
                steps[step][0](c, steps[step][2])


def sum_devices(dp, frame, given):
    rows = given.shape[0]
    n_core, n_y, n_x, n_z = factors(dp, frame)
    sizes = (n_core, n_x * n_y, n_z)
    vmem = pl.BlockSpec(memory_space=pltpu.VMEM)
    scratch, count = [pltpu.VMEM(given.shape, BF16)], rows
    for size in sizes:
        count //= size
        scratch.append(pltpu.VMEM((max(size - 1, 1), count, LANES), BF16))
    chunks = len(chunk_bounds(rows, dp * frame))
    sems = pltpu.SemaphoreType.DMA((chunks, len(sizes), max(max(sizes) - 1, 1)))
    return pl.pallas_call(
        functools.partial(sum_kernel, dp, frame),
        out_shape=jax.ShapeDtypeStruct(given.shape, BF16),
        in_specs=[vmem],
        out_specs=vmem,
        scratch_shapes=scratch + [sems] * 4,
        compiler_params=pltpu.CompilerParams(
            collective_id=1, has_side_effects=True, vmem_limit_bytes=32 * 2**20
        ),
        name="sum_devices",
    )(given)


def unpack_kernel(packed, g_in, g_gain, g_qkv, g_out, g_head):
    row = 0
    for ref in (g_in, g_qkv, g_out):
        height = ref.shape[0]
        for tile in range(ref.shape[1] // LANES):
            ref[:, tile * LANES : (tile + 1) * LANES] = packed[pl.ds(row, height), :].astype(F32)
            row += height
    for tile in range(g_head.shape[1] // LANES):
        small = packed[pl.ds(row, PACK), :].astype(F32)
        at = slice(tile * LANES, (tile + 1) * LANES)
        g_head[:, at] = small[0 : g_head.shape[0]]
        g_gain[at] = small[SUB]
        row += PACK


def unpack(packed, shapes):
    vmem = pl.BlockSpec(memory_space=pltpu.VMEM)
    return pl.pallas_call(
        unpack_kernel,
        out_shape=[jax.ShapeDtypeStruct(shape, F32) for shape in shapes],
        in_specs=[vmem],
        out_specs=[vmem] * len(shapes),
        compiler_params=pltpu.CompilerParams(vmem_limit_bytes=32 * 2**20),
        name="unpack",
    )(packed)


def body(
    dp,
    frame,
    features,
    vis_block,
    vis_count,
    query_frame,
    query_block,
    query_cell,
    cotangent,
    w_in,
    gain,
    w_qkv,
    w_out,
    w_head,
):
    hid = w_in.shape[1]
    cot = jnp.swapaxes(cotangent[0], 1, 2)
    picked, patches = pick(features, vis_block, vis_count, query_frame, query_block, query_cell)
    prepared = correlate(
        frame, picked, patches, cot, gain.reshape(1, hid), w_in, w_qkv, w_out, w_head
    )
    rows = packed_rows((w_in.shape, w_qkv.shape, w_out.shape, (PACK, hid)), dp * frame)
    packed = layer(rows, prepared, w_qkv)
    summed = sum_devices(dp, frame, packed)
    return tuple(unpack(summed, (w_in.shape, gain.shape, w_qkv.shape, w_out.shape, w_head.shape)))


def solution(mesh):
    in_specs = (
        P("dp", "frame", None, None, None),
        P("dp", None, "frame", None),
        P("dp", None, "frame"),
        P("dp", None),
        P("dp", None),
        P("dp", None),
        P("dp", None, "frame", None),
        P(),
        P(),
        P(),
        P(),
        P(),
    )
    out_specs = (P(), P(), P(), P(), P())
    run = functools.partial(body, mesh.shape["dp"], mesh.shape["frame"])
    return jax.shard_map(run, mesh=mesh, in_specs=in_specs, out_specs=out_specs, check_vma=False)
```

```python
import functools

import jax
import jax.numpy as jnp
from jax import lax
from jax.experimental import pallas as pl
from jax.experimental.pallas import tpu as pltpu
from jax.sharding import PartitionSpec as P

HEADS = 8
LANES = 128
SUB = 8
PACK = 16
CHUNKS = 3
MESH = pl.DeviceIdType.MESH
F32 = jnp.float32
BF16 = jnp.bfloat16


def dot_nn(left, right):
    return lax.dot_general(left, right, (((1,), (0,)), ((), ())), preferred_element_type=F32)


def dot_nt(left, right):
    return lax.dot_general(left, right, (((1,), (1,)), ((), ())), preferred_element_type=F32)


def dot_tn(left, right):
    return lax.dot_general(left, right, (((0,), (0,)), ((), ())), preferred_element_type=F32)


def pick_kernel(
    feats, vis_block, vis_count, q_frame, q_block, q_cell, queries, patches,
    s_block, s_count, s_frame, s_qblock, s_cell, tiles, picked, i_sem, p_sem, q_sem,
):
    fr_dev, cells, width = feats.shape[1], feats.shape[3], feats.shape[4]
    slots, groups = vis_block.shape[2], vis_block.shape[3]
    tracks = q_frame.shape[1]
    first = lax.axis_index("frame") * fr_dev
    loads = [
        pltpu.make_async_copy(src, dst, i_sem.at[i])
        for i, (src, dst) in enumerate(
            (
                (q_frame, s_frame),
                (q_block, s_qblock),
                (q_cell, s_cell),
                (vis_block, s_block),
                (vis_count, s_count),
            )
        )
    ]
    for load in loads:
        load.start()
    for load in loads[:3]:
        load.wait()

    @pl.loop(0, tracks // SUB)
    def _(step):
        for i in range(SUB):
            t = step * SUB + i
            local = jnp.clip(s_frame[0, t] - first, 0, fr_dev - 1)
            base = pl.multiple_of(lax.div(s_cell[0, t], PACK) * PACK, PACK)
            pltpu.make_async_copy(
                feats.at[0, local, s_qblock[0, t], pl.ds(base, PACK), :], tiles.at[t], q_sem
            ).start()

    for load in loads[3:]:
        load.wait()
    for g in range(groups):
        for f in range(fr_dev):
            for k in range(slots):
                pltpu.make_async_copy(
                    feats.at[0, f, s_block[0, f, k, g]],
                    patches.at[g, f, pl.ds(k * cells, cells)],
                    p_sem,
                ).start()

    row_id = lax.broadcasted_iota(jnp.int32, (PACK, width), 0)
    pltpu.make_async_copy(tiles, tiles, q_sem).wait()

    @pl.loop(0, tracks // SUB)
    def _(step):
        for i in range(SUB):
            t = step * SUB + i
            local = s_frame[0, t] - first
            inside = jnp.logical_and(local >= 0, local < fr_dev)
            row = jnp.where(inside, lax.rem(s_cell[0, t], PACK), PACK)
            kept = jnp.where(row_id == row, tiles[t].astype(F32), 0.0)
            picked[pl.ds(t, 1), :] = jnp.sum(kept, axis=0, keepdims=True)

    queries[...] = picked[...].astype(BF16)
    pltpu.make_async_copy(patches, patches, p_sem).wait()
    for g in range(groups):
        for f in range(fr_dev):
            for k in range(slots):

                @pl.when(k >= s_count[0, f, g])
                def _(g=g, f=f, k=k):
                    patches[g, f, k * cells : (k + 1) * cells] = jnp.zeros((cells, width), BF16)


def pick(feats, vis_block, vis_count, q_frame, q_block, q_cell):
    fr_dev, cells, width = feats.shape[1], feats.shape[3], feats.shape[4]
    groups, slots = vis_block.shape[1], vis_block.shape[3]
    tracks = q_frame.shape[1]
    vis_block = jnp.transpose(vis_block, (0, 2, 3, 1))
    vis_count = jnp.transpose(vis_count, (0, 2, 1))
    hbm = pl.BlockSpec(memory_space=pltpu.HBM)
    vmem = pl.BlockSpec(memory_space=pltpu.VMEM)
    arrays = (vis_block, vis_count, q_frame, q_block, q_cell)
    return pl.pallas_call(
        pick_kernel,
        out_shape=[
            jax.ShapeDtypeStruct((tracks, width), BF16),
            jax.ShapeDtypeStruct((groups, fr_dev, slots * cells, width), BF16),
        ],
        in_specs=[hbm] * 6,
        out_specs=[vmem, vmem],
        scratch_shapes=[pltpu.SMEM(array.shape, jnp.int32) for array in arrays]
        + [
            pltpu.VMEM((tracks, PACK, width), BF16),
            pltpu.VMEM((tracks, width), F32),
            pltpu.SemaphoreType.DMA((5,)),
            pltpu.SemaphoreType.DMA,
            pltpu.SemaphoreType.DMA,
        ],
        compiler_params=pltpu.CompilerParams(vmem_limit_bytes=60 * 2**20),
        name="pick",
    )(feats, *arrays)


def spread_cotangent(cot, tokens):
    outs, frames, tracks = cot.shape
    block = frames * SUB
    token = lax.broadcasted_iota(jnp.int32, (tracks, tokens), 1)
    track = lax.broadcasted_iota(jnp.int32, (tracks, tokens), 0)
    wanted = lax.div(token, block) * SUB + lax.rem(token, SUB)
    choose = jnp.where(track == wanted, 1.0, 0.0).astype(BF16)
    spread = dot_nn(cot[...].reshape(outs * frames, tracks), choose)
    token = lax.broadcasted_iota(jnp.int32, (frames, tokens), 1)
    row = lax.broadcasted_iota(jnp.int32, (frames, tokens), 0)
    here = lax.div(lax.rem(token, block), SUB) == row
    return [
        jnp.sum(
            jnp.where(here, spread[o * frames : (o + 1) * frames], 0.0), axis=0, keepdims=True
        )
        for o in range(outs)
    ]


def exchange(
    n, plan,
    picked, patches, cot, gain, w_in, w_qkv, w_out, w_head,
    out, w_in_t, w_qkv_t, w_out_t, ct, gain_col, d_y, datt_t,
    q_recv, c_send, head_pad, ct_pad, q_ssem, q_rsem, c_ssem, c_rsem,
):
    me = lax.axis_index("frame")
    groups, fr_dev, _, width = patches.shape
    in_group = picked.shape[0] // groups
    own = groups // n
    barrier = pltpu.get_barrier_semaphore()
    greeted = [{"frame": lax.rem(me + j, n)} for j in range(1, n)]
    for size, digit, device in plan:
        greeted += [device(lax.rem(digit + j, size)) for j in range(1, size)]
    for peer in greeted:
        pl.semaphore_signal(barrier, inc=1, device_id=peer, device_id_type=MESH)
    w_in_t[...] = w_in[...].T
    w_out_t[...] = w_out[...].T
    pl.semaphore_wait(barrier, len(greeted))
    copies = []
    for j in range(1, n):
        copy = pltpu.make_async_remote_copy(
            src_ref=picked,
            dst_ref=q_recv.at[j - 1],
            send_sem=q_ssem.at[j - 1],
            recv_sem=q_rsem.at[j - 1],
            device_id={"frame": lax.rem(me + j, n)},
            device_id_type=MESH,
        )
        copy.start()
        copies.append(copy)
    w_qkv_t[...] = w_qkv[...].T
    for copy in copies:
        copy.wait()
    total = picked[...].astype(F32)
    for j in range(1, n):
        total = total + q_recv[j - 1].astype(F32)
    query = total.astype(BF16)

    scale = width ** (-0.5)
    for g in range(groups):
        q_rows = query[g * in_group : (g + 1) * in_group]
        for f in range(fr_dev):
            corr = dot_nt(q_rows, patches[g, f]) * scale
            c_send[g // own, g % own, f] = corr.astype(BF16)
    copies = []
    for j in range(1, n):
        peer = lax.rem(me + j, n)
        copy = pltpu.make_async_remote_copy(
            src_ref=c_send.at[peer],
            dst_ref=out.at[me],
            send_sem=c_ssem.at[j - 1],
            recv_sem=c_rsem.at[j - 1],
            device_id={"frame": peer},
            device_id_type=MESH,
        )
        copy.start()
        copies.append(copy)
    out[me] = c_send[me]

    head_pad[...] = jnp.zeros_like(head_pad)
    head_pad[0 : w_head.shape[0], :] = w_head[...].astype(F32)
    ct_pad[...] = jnp.zeros_like(ct_pad)
    for o, row in enumerate(spread_cotangent(cot, ct_pad.shape[1])):
        ct_pad[o : o + 1, :] = row
    ct_rows = ct_pad[...].astype(BF16)
    ct[...] = ct_rows
    dy = dot_tn(head_pad[...].astype(BF16), ct_rows)
    d_y[...] = dy
    datt_t[...] = dot_nn(w_out[...], dy.astype(BF16)).astype(BF16)
    gain_col[...] = jnp.broadcast_to(gain[...], (LANES, gain.shape[1])).T[:, 0:1]
    for copy in copies:
        copy.wait()


def layer(
    corr, w_in_t, w_qkv_t, w_out_t, ct, gain, dy_ref, datt_t, w_qkv, packed, qkv_t, dqkv_t, att_t, ready
):
    n, own, fr_dev, in_group, width = corr.shape
    frames = n * fr_dev
    hid = w_in_t.shape[0]
    size = hid // HEADS
    block = frames * SUB
    halves = in_group // SUB
    tokens = own * halves * block

    c32 = corr[...].astype(F32)
    parts = []
    for g in range(own):
        piece = c32[:, g].reshape(frames, halves, SUB, width)
        for half in range(halves):
            parts.append(piece[:, half].reshape(block, width))
    rows32 = jnp.concatenate(parts, axis=0)
    rows = rows32.astype(BF16)
    rows_t = rows32.T.astype(BF16)

    x_zero = dot_nn(w_in_t[...], rows_t)
    centred = x_zero - jnp.mean(x_zero, axis=0, keepdims=True)
    inv_std = lax.rsqrt(jnp.mean(centred * centred, axis=0, keepdims=True) + 1e-05)
    normed = centred * inv_std
    gain_col = gain[...]
    hidden = (normed * gain_col).astype(BF16)
    qkv_t[...] = dot_nn(w_qkv_t[...], hidden).astype(BF16)

    ct_rows = ct[...]
    d_y = dy_ref[...]
    d_y16 = d_y.astype(BF16)

    scale = size ** (-0.5)
    key_id = lax.broadcasted_iota(jnp.int32, (block, block), 0)
    query_id = lax.broadcasted_iota(jnp.int32, (block, block), 1)
    same = lax.rem(key_id, SUB) == lax.rem(query_id, SUB)
    to_exp2 = scale * 1.4426950408889634

    for b in range(tokens // block):
        at = pl.ds(b * block, block)
        for head in range(HEADS):
            mine = pl.ds(head * size, size)
            q = qkv_t[mine, at]
            k = qkv_t[pl.ds(hid + head * size, size), at]
            v = qkv_t[pl.ds(2 * hid + head * size, size), at]
            d_att = datt_t[mine, at]
            scores = jnp.where(same, dot_tn(k, q), -1e30)
            top = jnp.max(scores, axis=0, keepdims=True)
            powers = jnp.exp2((scores - top) * to_exp2)
            probs = powers * (1.0 / jnp.sum(powers, axis=0, keepdims=True))
            probs16 = probs.astype(BF16)
            att_t[mine, at] = dot_nn(v, probs16).astype(BF16)
            d_v = dot_nt(d_att, probs16)
            d_probs = dot_tn(v, d_att).astype(BF16).astype(F32)
            weighted = probs * d_probs
            d_scores = weighted - probs * jnp.sum(weighted, axis=0, keepdims=True)
            d_scores = d_scores.astype(BF16)
            d_q = dot_nn(k, d_scores) * scale
            d_k = dot_nt(q, d_scores) * scale
            dqkv_t[mine, at] = d_q.astype(BF16)
            dqkv_t[pl.ds(hid + head * size, size), at] = d_k.astype(BF16)
            dqkv_t[pl.ds(2 * hid + head * size, size), at] = d_v.astype(BF16)

    def put(row, value):
        for tile in range(value.shape[1] // LANES):
            packed[pl.ds(row, value.shape[0]), :] = value[
                :, tile * LANES : (tile + 1) * LANES
            ].astype(BF16)
            row += value.shape[0]
        ready(row)
        return row

    row = 0
    att = att_t[...]
    for tile in range(hid // LANES):
        row = put(row, dot_nt(att, d_y16[tile * LANES : (tile + 1) * LANES]))
    for tile in range(3 * hid // LANES):
        row = put(row, dot_nt(hidden, dqkv_t[tile * LANES : (tile + 1) * LANES, :]))
    y_out = (x_zero + dot_nn(w_out_t[...], att)).astype(BF16)
    d_hidden = dot_nn(w_qkv[...], dqkv_t[...])
    product = d_hidden * normed
    d_norm = d_hidden * gain_col
    d_x = (
        inv_std
        * (
            d_norm
            - jnp.mean(d_norm, axis=0, keepdims=True)
            - normed * jnp.mean(d_norm * normed, axis=0, keepdims=True)
        )
        + d_y
    )
    row = put(row, dot_nt(rows_t, d_x.astype(BF16)))
    high = product.astype(BF16)
    low = (product - high.astype(F32)).astype(BF16)
    picks = (lax.broadcasted_iota(jnp.int32, (PACK, tokens), 0) == SUB).astype(F32).astype(BF16)
    row = put(row, dot_nt(ct_rows, y_out) + dot_nt(picks, high) + dot_nt(picks, low))
    if row < packed.shape[0]:
        packed[pl.ds(row, packed.shape[0] - row), :] = jnp.zeros(
            (packed.shape[0] - row, LANES), BF16
        )
    ready(packed.shape[0])


def packed_rows(shapes, devices):
    rows = sum(-(-r // PACK) * PACK * (c // LANES) for r, c in shapes)
    step = PACK * devices
    return -(-rows // step) * step


def factors(dp, frame):
    core = 2 if frame % 2 == 0 else 1
    mid = frame // core
    low = mid if dp % mid == 0 else 1
    return core, mid, low, dp // low


def stages(dp, frame):
    n_core, n_y, n_x, n_z = factors(dp, frame)
    me_d, me_f = lax.axis_index("dp"), lax.axis_index("frame")
    core, y = lax.rem(me_f, n_core), lax.div(me_f, n_core)
    x, z = lax.rem(me_d, n_x), lax.div(me_d, n_x)
    swap = core if n_core == 2 and n_x == n_y else 0

    def device(core_at, y_at, x_at, z_at):
        return (z_at * n_x + x_at, y_at * n_core + core_at)

    return (
        (n_core, core, lambda d: device(d, y, x, z)),
        (n_x * n_y, y * n_x + x, lambda d: device(core, lax.div(d, n_x), lax.rem(d, n_x), z)),
        (n_z, z, lambda d: device(core, y, x, d)),
    )


def chunk_bounds(rows, devices):
    units = rows // (PACK * devices)
    chunks = min(CHUNKS, units)
    sizes = [(units + chunks - 1 - c) // chunks * PACK * devices for c in range(chunks)]
    return [(sum(sizes[:c]), sizes[c]) for c in range(chunks)]


def device_sum(plan, bounds, given, out, work, recvs, rs_send, rs_recv, ag_send, ag_recv):
    last = len(plan) - 1
    begins = [begin for begin, _ in bounds]
    counts = [count for _, count in bounds]
    offsets = [begin for begin, _ in bounds]
    flying = [[] for _ in bounds]

    def scatter_start(c, at):
        size, digit, device = plan[at]
        source = given if at == 0 else work
        part = counts[c] // size
        offsets[c] //= size
        for j in range(1, size):
            peer = lax.rem(digit + j, size)
            copy = pltpu.make_async_remote_copy(
                src_ref=source.at[pl.ds(pl.multiple_of(begins[c] + peer * part, PACK), part)],
                dst_ref=recvs[at].at[j - 1, pl.ds(offsets[c], part)],
                send_sem=rs_send.at[c, at, j - 1],
                recv_sem=rs_recv.at[c, at, j - 1],
                device_id=device(peer),
                device_id_type=MESH,
            )
            copy.start()
            flying[c].append(copy)

    def scatter_end(c, at):
        size, digit, device = plan[at]
        source = given if at == 0 else work
        target = out if at == last else work
        part = counts[c] // size
        for copy in flying[c]:
            copy.wait()
        flying[c] = []
        begins[c] = pl.multiple_of(begins[c] + digit * part, PACK)
        counts[c] = part
        total = source[pl.ds(begins[c], part), :].astype(F32)
        for j in range(1, size):
            total = total + recvs[at][j - 1, pl.ds(offsets[c], part), :].astype(F32)
        target[pl.ds(begins[c], part), :] = total.astype(BF16)

    def gather_start(c, at):
        size, digit, device = plan[at]
        for j in range(1, size):
            here = out.at[pl.ds(begins[c], counts[c])]
            copy = pltpu.make_async_remote_copy(
                src_ref=here,
                dst_ref=here,
                send_sem=ag_send.at[c, at, j - 1],
                recv_sem=ag_recv.at[c, at, j - 1],
                device_id=device(lax.rem(digit + j, size)),
                device_id_type=MESH,
            )
            copy.start()
            flying[c].append(copy)

    def gather_end(c, at):
        size, digit, device = plan[at]
        for copy in flying[c]:
            copy.wait()
        flying[c] = []
        begins[c] = pl.multiple_of(begins[c] - digit * counts[c], PACK)
        counts[c] = counts[c] * size

    steps = [(scatter_start, scatter_end, at) for at in range(last + 1)]
    steps += [(gather_start, gather_end, at) for at in range(last, -1, -1)]
    started = []

    def ready(row):
        for c, (begin, count) in enumerate(bounds):
            if begin + count <= row and c not in started:
                started.append(c)
                scatter_start(c, 0)

    def finish():
        for step in range(1, len(steps) + 1):
            for c in range(len(bounds)):
                steps[step - 1][1](c, steps[step - 1][2])
                if step < len(steps):
                    steps[step][0](c, steps[step][2])

    return ready, finish


def train_kernel(
    dp, frame,
    picked, patches, cot, gain, w_in, w_qkv, w_out, w_head,
    summed,
    corr, w_in_t, w_qkv_t, w_out_t, ct, gain_col, d_y, datt_t,
    q_recv, c_send, head_pad, ct_pad, q_ssem, q_rsem, c_ssem, c_rsem,
    qkv_t, dqkv_t, att_t,
    given, work, r0, r1, r2, rs_send, rs_recv, ag_send, ag_recv,
):
    plan = stages(dp, frame)
    bounds = chunk_bounds(given.shape[0], dp * frame)
    exchange(
        frame, plan, picked, patches, cot, gain, w_in, w_qkv, w_out, w_head,
        corr, w_in_t, w_qkv_t, w_out_t, ct, gain_col, d_y, datt_t,
        q_recv, c_send, head_pad, ct_pad, q_ssem, q_rsem, c_ssem, c_rsem,
    )
    ready, finish = device_sum(
        plan, bounds, given, summed, work, (r0, r1, r2), rs_send, rs_recv, ag_send, ag_recv
    )
    layer(
        corr, w_in_t, w_qkv_t, w_out_t, ct, gain_col, d_y, datt_t, w_qkv,
        given, qkv_t, dqkv_t, att_t, ready,
    )
    finish()


def train(dp, frame, rows, picked, patches, cot, gain, w_in, w_qkv, w_out, w_head):
    groups, fr_dev, cells, _ = patches.shape
    tracks, width = picked.shape
    hid = w_in.shape[1]
    tokens = cot.shape[1] * cot.shape[2]
    shape = (frame, groups // frame, fr_dev, tracks // groups, cells)
    vmem = pl.BlockSpec(memory_space=pltpu.VMEM)
    peers = pltpu.SemaphoreType.DMA((frame - 1,))
    scratch = [
        pltpu.VMEM(*item)
        for item in (
            (shape, BF16),
            (w_in.shape[::-1], BF16),
            (w_qkv.shape[::-1], BF16),
            (w_out.shape[::-1], BF16),
            ((PACK, tokens), BF16),
            ((hid, 1), F32),
            ((hid, tokens), F32),
            ((hid, tokens), BF16),
            ((frame - 1, tracks, width), BF16),
            (shape, BF16),
            ((PACK, hid), F32),
            ((PACK, tokens), F32),
        )
    ]
    scratch += [peers] * 4
    scratch += [
        pltpu.VMEM((3 * hid, tokens), BF16),
        pltpu.VMEM((3 * hid, tokens), BF16),
        pltpu.VMEM((hid, tokens), BF16),
    ]
    n_core, n_y, n_x, n_z = factors(dp, frame)
    sizes = (n_core, n_x * n_y, n_z)
    scratch += [pltpu.VMEM((rows, LANES), BF16)] * 2
    count = rows
    for size in sizes:
        count //= size
        scratch.append(pltpu.VMEM((max(size - 1, 1), count, LANES), BF16))
    chunks = len(chunk_bounds(rows, dp * frame))
    scratch += [pltpu.SemaphoreType.DMA((chunks, len(sizes), max(max(sizes) - 1, 1)))] * 4
    return pl.pallas_call(
        functools.partial(train_kernel, dp, frame),
        out_shape=jax.ShapeDtypeStruct((rows, LANES), BF16),
        in_specs=[vmem] * 8,
        out_specs=vmem,
        scratch_shapes=scratch,
        compiler_params=pltpu.CompilerParams(
            collective_id=0, has_side_effects=True, vmem_limit_bytes=48 * 2**20
        ),
        name="train",
    )(picked, patches, cot, gain, w_in, w_qkv, w_out, w_head)


def unpack_kernel(packed, g_in, g_gain, g_qkv, g_out, g_head):
    row = 0
    for ref in (g_out, g_qkv, g_in):
        height = ref.shape[0]
        for tile in range(ref.shape[1] // LANES):
            ref[:, tile * LANES : (tile + 1) * LANES] = packed[pl.ds(row, height), :].astype(F32)
            row += height
    for tile in range(g_head.shape[1] // LANES):
        small = packed[pl.ds(row, PACK), :].astype(F32)
        at = slice(tile * LANES, (tile + 1) * LANES)
        g_head[:, at] = small[0 : g_head.shape[0]]
        g_gain[at] = small[SUB]
        row += PACK


def unpack(packed, shapes):
    vmem = pl.BlockSpec(memory_space=pltpu.VMEM)
    return pl.pallas_call(
        unpack_kernel,
        out_shape=[jax.ShapeDtypeStruct(shape, F32) for shape in shapes],
        in_specs=[vmem],
        out_specs=[vmem] * len(shapes),
        compiler_params=pltpu.CompilerParams(vmem_limit_bytes=32 * 2**20),
        name="unpack",
    )(packed)


def body(
    dp,
    frame,
    features,
    vis_block,
    vis_count,
    query_frame,
    query_block,
    query_cell,
    cotangent,
    w_in,
    gain,
    w_qkv,
    w_out,
    w_head,
):
    hid = w_in.shape[1]
    cot = jnp.swapaxes(cotangent[0], 1, 2)
    picked, patches = pick(features, vis_block, vis_count, query_frame, query_block, query_cell)
    rows = packed_rows((w_in.shape, w_qkv.shape, w_out.shape, (PACK, hid)), dp * frame)
    summed = train(
        dp, frame, rows, picked, patches, cot, gain.reshape(1, hid), w_in, w_qkv, w_out, w_head
    )
    return tuple(unpack(summed, (w_in.shape, gain.shape, w_qkv.shape, w_out.shape, w_head.shape)))


def solution(mesh):
    in_specs = (
        P("dp", "frame", None, None, None),
        P("dp", None, "frame", None),
        P("dp", None, "frame"),
        P("dp", None),
        P("dp", None),
        P("dp", None),
        P("dp", None, "frame", None),
        P(),
        P(),
        P(),
        P(),
        P(),
    )
    out_specs = (P(), P(), P(), P(), P())
    run = functools.partial(body, mesh.shape["dp"], mesh.shape["frame"])
    return jax.shard_map(run, mesh=mesh, in_specs=in_specs, out_specs=out_specs, check_vma=False)
```

```python
import functools

import jax
import jax.numpy as jnp
from jax import lax
from jax.experimental import pallas as pl
from jax.experimental.pallas import tpu as pltpu
from jax.sharding import PartitionSpec as P

HEADS = 8
LANES = 128
SUB = 8
PACK = 16
CHUNKS = 3
LOOP = 32
MESH = pl.DeviceIdType.MESH
F32 = jnp.float32
BF16 = jnp.bfloat16


def dot_nn(left, right):
    return lax.dot_general(left, right, (((1,), (0,)), ((), ())), preferred_element_type=F32)


def dot_nt(left, right):
    return lax.dot_general(left, right, (((1,), (1,)), ((), ())), preferred_element_type=F32)


def dot_tn(left, right):
    return lax.dot_general(left, right, (((0,), (0,)), ((), ())), preferred_element_type=F32)


def pick_kernel(
    feats, vis_block, vis_count, q_frame, q_block, q_cell, queries, patches,
    s_block, s_count, s_frame, s_qblock, s_cell, tiles, picked, i_sem, p_sem, q_sem,
):
    fr_dev, cells, width = feats.shape[1], feats.shape[3], feats.shape[4]
    slots, groups = vis_block.shape[2], vis_block.shape[3]
    tracks = q_frame.shape[1]
    first = lax.axis_index("frame") * fr_dev
    loads = [
        pltpu.make_async_copy(src, dst, i_sem.at[i])
        for i, (src, dst) in enumerate(
            (
                (q_frame, s_frame),
                (q_block, s_qblock),
                (q_cell, s_cell),
                (vis_block, s_block),
                (vis_count, s_count),
            )
        )
    ]
    for load in loads:
        load.start()
    for load in loads[:3]:
        load.wait()

    @pl.loop(0, tracks // SUB)
    def _(step):
        for i in range(SUB):
            t = step * SUB + i
            local = jnp.clip(s_frame[0, t] - first, 0, fr_dev - 1)
            base = pl.multiple_of(lax.div(s_cell[0, t], PACK) * PACK, PACK)
            pltpu.make_async_copy(
                feats.at[0, local, s_qblock[0, t], pl.ds(base, PACK), :], tiles.at[t], q_sem
            ).start()

    for load in loads[3:]:
        load.wait()
    for g in range(groups):
        for f in range(fr_dev):
            for k in range(slots):
                pltpu.make_async_copy(
                    feats.at[0, f, s_block[0, f, k, g]],
                    patches.at[g, f, pl.ds(k * cells, cells)],
                    p_sem,
                ).start()

    row_id = lax.broadcasted_iota(jnp.int32, (PACK, width), 0)
    pltpu.make_async_copy(tiles, tiles, q_sem).wait()

    @pl.loop(0, tracks // LOOP)
    def _(step):
        for i in range(LOOP):
            t = step * LOOP + i
            local = s_frame[0, t] - first
            inside = jnp.logical_and(local >= 0, local < fr_dev)
            row = jnp.where(inside, lax.rem(s_cell[0, t], PACK), PACK)
            kept = jnp.where(row_id == row, tiles[t].astype(F32), 0.0)
            picked[pl.ds(t, 1), :] = jnp.sum(kept, axis=0, keepdims=True)

    queries[...] = picked[...].astype(BF16)
    pltpu.make_async_copy(patches, patches, p_sem).wait()
    for g in range(groups):
        for f in range(fr_dev):
            for k in range(slots):

                @pl.when(k >= s_count[0, f, g])
                def _(g=g, f=f, k=k):
                    patches[g, f, k * cells : (k + 1) * cells] = jnp.zeros((cells, width), BF16)


def pick(feats, vis_block, vis_count, q_frame, q_block, q_cell):
    fr_dev, cells, width = feats.shape[1], feats.shape[3], feats.shape[4]
    groups, slots = vis_block.shape[1], vis_block.shape[3]
    tracks = q_frame.shape[1]
    vis_block = jnp.transpose(vis_block, (0, 2, 3, 1))
    vis_count = jnp.transpose(vis_count, (0, 2, 1))
    hbm = pl.BlockSpec(memory_space=pltpu.HBM)
    vmem = pl.BlockSpec(memory_space=pltpu.VMEM)
    arrays = (vis_block, vis_count, q_frame, q_block, q_cell)
    return pl.pallas_call(
        pick_kernel,
        out_shape=[
            jax.ShapeDtypeStruct((tracks, width), BF16),
            jax.ShapeDtypeStruct((groups, fr_dev, slots * cells, width), BF16),
        ],
        in_specs=[hbm] * 6,
        out_specs=[vmem, vmem],
        scratch_shapes=[pltpu.SMEM(array.shape, jnp.int32) for array in arrays]
        + [
            pltpu.VMEM((tracks, PACK, width), BF16),
            pltpu.VMEM((tracks, width), F32),
            pltpu.SemaphoreType.DMA((5,)),
            pltpu.SemaphoreType.DMA,
            pltpu.SemaphoreType.DMA,
        ],
        compiler_params=pltpu.CompilerParams(vmem_limit_bytes=60 * 2**20),
        name="pick",
    )(feats, *arrays)


def spread_cotangent(cot, tokens):
    outs, frames, tracks = cot.shape
    block = frames * SUB
    token = lax.broadcasted_iota(jnp.int32, (tracks, tokens), 1)
    track = lax.broadcasted_iota(jnp.int32, (tracks, tokens), 0)
    wanted = lax.div(token, block) * SUB + lax.rem(token, SUB)
    choose = jnp.where(track == wanted, 1.0, 0.0).astype(BF16)
    spread = dot_nn(cot[...].reshape(outs * frames, tracks), choose)
    token = lax.broadcasted_iota(jnp.int32, (frames, tokens), 1)
    row = lax.broadcasted_iota(jnp.int32, (frames, tokens), 0)
    here = lax.div(lax.rem(token, block), SUB) == row
    return [
        jnp.sum(
            jnp.where(here, spread[o * frames : (o + 1) * frames], 0.0), axis=0, keepdims=True
        )
        for o in range(outs)
    ]


def exchange(
    n, plan,
    picked, patches, cot, gain, w_in, w_qkv, w_out, w_head,
    out, w_in_t, w_qkv_t, w_out_t, ct, gain_col, d_y, datt_t,
    q_recv, c_send, head_pad, ct_pad, q_ssem, q_rsem, c_ssem, c_rsem,
):
    me = lax.axis_index("frame")
    groups, fr_dev, _, width = patches.shape
    in_group = picked.shape[0] // groups
    own = groups // n
    barrier = pltpu.get_barrier_semaphore()
    greeted = [{"frame": lax.rem(me + j, n)} for j in range(1, n)]
    for size, digit, device in plan:
        greeted += [device(lax.rem(digit + j, size)) for j in range(1, size)]
    for peer in greeted:
        pl.semaphore_signal(barrier, inc=1, device_id=peer, device_id_type=MESH)
    w_in_t[...] = w_in[...].T
    w_out_t[...] = w_out[...].T
    pl.semaphore_wait(barrier, len(greeted))
    copies = []
    for j in range(1, n):
        copy = pltpu.make_async_remote_copy(
            src_ref=picked,
            dst_ref=q_recv.at[j - 1],
            send_sem=q_ssem.at[j - 1],
            recv_sem=q_rsem.at[j - 1],
            device_id={"frame": lax.rem(me + j, n)},
            device_id_type=MESH,
        )
        copy.start()
        copies.append(copy)
    w_qkv_t[...] = w_qkv[...].T
    for copy in copies:
        copy.wait()
    total = picked[...].astype(F32)
    for j in range(1, n):
        total = total + q_recv[j - 1].astype(F32)
    query = total.astype(BF16)

    scale = width ** (-0.5)
    for g in range(groups):
        q_rows = query[g * in_group : (g + 1) * in_group]
        for f in range(fr_dev):
            corr = dot_nt(q_rows, patches[g, f]) * scale
            c_send[g // own, g % own, f] = corr.astype(BF16)
    copies = []
    for j in range(1, n):
        peer = lax.rem(me + j, n)
        copy = pltpu.make_async_remote_copy(
            src_ref=c_send.at[peer],
            dst_ref=out.at[me],
            send_sem=c_ssem.at[j - 1],
            recv_sem=c_rsem.at[j - 1],
            device_id={"frame": peer},
            device_id_type=MESH,
        )
        copy.start()
        copies.append(copy)
    out[me] = c_send[me]

    head_pad[...] = jnp.zeros_like(head_pad)
    head_pad[0 : w_head.shape[0], :] = w_head[...].astype(F32)
    ct_pad[...] = jnp.zeros_like(ct_pad)
    for o, row in enumerate(spread_cotangent(cot, ct_pad.shape[1])):
        ct_pad[o : o + 1, :] = row
    ct_rows = ct_pad[...].astype(BF16)
    ct[...] = ct_rows
    dy = dot_tn(head_pad[...].astype(BF16), ct_rows)
    d_y[...] = dy
    datt_t[...] = dot_nn(w_out[...], dy.astype(BF16)).astype(BF16)
    gain_col[...] = jnp.broadcast_to(gain[...].reshape(1, -1), (LANES, gain.shape[0])).T[:, 0:1]
    for copy in copies:
        copy.wait()


def layer(
    corr, w_in_t, w_qkv_t, w_out_t, ct, gain, dy_ref, datt_t, w_qkv, packed, qkv_t, dqkv_t, att_t, ready
):
    n, own, fr_dev, in_group, width = corr.shape
    frames = n * fr_dev
    hid = w_in_t.shape[0]
    size = hid // HEADS
    block = frames * SUB
    halves = in_group // SUB
    tokens = own * halves * block

    c32 = corr[...].astype(F32)
    parts = []
    for g in range(own):
        piece = c32[:, g].reshape(frames, halves, SUB, width)
        for half in range(halves):
            parts.append(piece[:, half].reshape(block, width))
    rows32 = jnp.concatenate(parts, axis=0)
    rows = rows32.astype(BF16)
    rows_t = rows32.T.astype(BF16)

    x_zero = dot_nn(w_in_t[...], rows_t)
    centred = x_zero - jnp.mean(x_zero, axis=0, keepdims=True)
    inv_std = lax.rsqrt(jnp.mean(centred * centred, axis=0, keepdims=True) + 1e-05)
    normed = centred * inv_std
    gain_col = gain[...]
    hidden = (normed * gain_col).astype(BF16)
    qkv_t[...] = dot_nn(w_qkv_t[...], hidden).astype(BF16)

    ct_rows = ct[...]
    d_y = dy_ref[...]
    d_y16 = d_y.astype(BF16)

    scale = size ** (-0.5)
    key_id = lax.broadcasted_iota(jnp.int32, (block, block), 0)
    query_id = lax.broadcasted_iota(jnp.int32, (block, block), 1)
    same = lax.rem(key_id, SUB) == lax.rem(query_id, SUB)
    to_exp2 = scale * 1.4426950408889634

    for b in range(tokens // block):
        at = pl.ds(b * block, block)
        for head in range(HEADS):
            mine = pl.ds(head * size, size)
            q = qkv_t[mine, at]
            k = qkv_t[pl.ds(hid + head * size, size), at]
            v = qkv_t[pl.ds(2 * hid + head * size, size), at]
            d_att = datt_t[mine, at]
            scores = jnp.where(same, dot_tn(k, q), -1e30)
            top = jnp.max(scores, axis=0, keepdims=True)
            powers = jnp.exp2((scores - top) * to_exp2)
            probs = powers * (1.0 / jnp.sum(powers, axis=0, keepdims=True))
            probs16 = probs.astype(BF16)
            att_t[mine, at] = dot_nn(v, probs16).astype(BF16)
            d_v = dot_nt(d_att, probs16)
            d_probs = dot_tn(v, d_att).astype(BF16).astype(F32)
            weighted = probs * d_probs
            d_scores = weighted - probs * jnp.sum(weighted, axis=0, keepdims=True)
            d_scores = d_scores.astype(BF16)
            d_q = dot_nn(k, d_scores) * scale
            d_k = dot_nt(q, d_scores) * scale
            dqkv_t[mine, at] = d_q.astype(BF16)
            dqkv_t[pl.ds(hid + head * size, size), at] = d_k.astype(BF16)
            dqkv_t[pl.ds(2 * hid + head * size, size), at] = d_v.astype(BF16)

    def put(row, value):
        for tile in range(value.shape[1] // LANES):
            packed[pl.ds(row, value.shape[0]), :] = value[
                :, tile * LANES : (tile + 1) * LANES
            ].astype(BF16)
            row += value.shape[0]
        ready(row)
        return row

    row = 0
    att = att_t[...]
    for tile in range(hid // LANES):
        row = put(row, dot_nt(att, d_y16[tile * LANES : (tile + 1) * LANES]))
    for tile in range(3 * hid // LANES):
        row = put(row, dot_nt(hidden, dqkv_t[tile * LANES : (tile + 1) * LANES, :]))
    y_out = (x_zero + dot_nn(w_out_t[...], att)).astype(BF16)
    d_hidden = dot_nn(w_qkv[...], dqkv_t[...])
    product = d_hidden * normed
    d_norm = d_hidden * gain_col
    d_x = (
        inv_std
        * (
            d_norm
            - jnp.mean(d_norm, axis=0, keepdims=True)
            - normed * jnp.mean(d_norm * normed, axis=0, keepdims=True)
        )
        + d_y
    )
    row = put(row, dot_nt(rows_t, d_x.astype(BF16)))
    high = product.astype(BF16)
    low = (product - high.astype(F32)).astype(BF16)
    picks = (lax.broadcasted_iota(jnp.int32, (PACK, tokens), 0) == SUB).astype(F32).astype(BF16)
    row = put(row, dot_nt(ct_rows, y_out) + dot_nt(picks, high) + dot_nt(picks, low))
    if row < packed.shape[0]:
        packed[pl.ds(row, packed.shape[0] - row), :] = jnp.zeros(
            (packed.shape[0] - row, LANES), BF16
        )
    ready(packed.shape[0])


def packed_rows(shapes, devices):
    rows = sum(-(-r // PACK) * PACK * (c // LANES) for r, c in shapes)
    step = PACK * devices
    return -(-rows // step) * step


def factors(dp, frame):
    core = 2 if frame % 2 == 0 else 1
    mid = frame // core
    low = mid if dp % mid == 0 else 1
    return core, mid, low, dp // low


def stages(dp, frame):
    n_core, n_y, n_x, n_z = factors(dp, frame)
    me_d, me_f = lax.axis_index("dp"), lax.axis_index("frame")
    core, y = lax.rem(me_f, n_core), lax.div(me_f, n_core)
    x, z = lax.rem(me_d, n_x), lax.div(me_d, n_x)
    swap = core if n_core == 2 and n_x == n_y else 0

    def device(core_at, y_at, x_at, z_at):
        return (z_at * n_x + x_at, y_at * n_core + core_at)

    return (
        (n_core, core, lambda d: device(d, y, x, z)),
        (n_x * n_y, y * n_x + x, lambda d: device(core, lax.div(d, n_x), lax.rem(d, n_x), z)),
        (n_z, z, lambda d: device(core, y, x, d)),
    )


def chunk_bounds(rows, devices):
    units = rows // (PACK * devices)
    chunks = min(CHUNKS, units)
    sizes = [(units + chunks - 1 - c) // chunks * PACK * devices for c in range(chunks)]
    return [(sum(sizes[:c]), sizes[c]) for c in range(chunks)]


def device_sum(plan, bounds, given, out, work, recvs, rs_send, rs_recv, ag_send, ag_recv):
    last = len(plan) - 1
    begins = [begin for begin, _ in bounds]
    counts = [count for _, count in bounds]
    offsets = [begin for begin, _ in bounds]
    flying = [[] for _ in bounds]

    def scatter_start(c, at):
        size, digit, device = plan[at]
        source = given if at == 0 else work
        part = counts[c] // size
        offsets[c] //= size
        for j in range(1, size):
            peer = lax.rem(digit + j, size)
            copy = pltpu.make_async_remote_copy(
                src_ref=source.at[pl.ds(pl.multiple_of(begins[c] + peer * part, PACK), part)],
                dst_ref=recvs[at].at[j - 1, pl.ds(offsets[c], part)],
                send_sem=rs_send.at[c, at, j - 1],
                recv_sem=rs_recv.at[c, at, j - 1],
                device_id=device(peer),
                device_id_type=MESH,
            )
            copy.start()
            flying[c].append(copy)

    def scatter_end(c, at):
        size, digit, device = plan[at]
        source = given if at == 0 else work
        target = out if at == last else work
        part = counts[c] // size
        for copy in flying[c]:
            copy.wait()
        flying[c] = []
        begins[c] = pl.multiple_of(begins[c] + digit * part, PACK)
        counts[c] = part
        total = source[pl.ds(begins[c], part), :].astype(F32)
        for j in range(1, size):
            total = total + recvs[at][j - 1, pl.ds(offsets[c], part), :].astype(F32)
        target[pl.ds(begins[c], part), :] = total.astype(BF16)

    def gather_start(c, at):
        size, digit, device = plan[at]
        for j in range(1, size):
            here = out.at[pl.ds(begins[c], counts[c])]
            copy = pltpu.make_async_remote_copy(
                src_ref=here,
                dst_ref=here,
                send_sem=ag_send.at[c, at, j - 1],
                recv_sem=ag_recv.at[c, at, j - 1],
                device_id=device(lax.rem(digit + j, size)),
                device_id_type=MESH,
            )
            copy.start()
            flying[c].append(copy)

    def gather_end(c, at):
        size, digit, device = plan[at]
        for copy in flying[c]:
            copy.wait()
        flying[c] = []
        begins[c] = pl.multiple_of(begins[c] - digit * counts[c], PACK)
        counts[c] = counts[c] * size

    steps = [(scatter_start, scatter_end, at) for at in range(last + 1)]
    steps += [(gather_start, gather_end, at) for at in range(last, -1, -1)]
    started = []

    def ready(row):
        for c, (begin, count) in enumerate(bounds):
            if begin + count <= row and c not in started:
                started.append(c)
                scatter_start(c, 0)

    def finish():
        for step in range(1, len(steps) + 1):
            for c in range(len(bounds)):
                steps[step - 1][1](c, steps[step - 1][2])
                if step < len(steps):
                    steps[step][0](c, steps[step][2])

    return ready, finish


def train_kernel(
    dp, frame,
    picked, patches, cot, gain, w_in, w_qkv, w_out, w_head,
    summed,
    corr, w_in_t, w_qkv_t, w_out_t, ct, gain_col, d_y, datt_t,
    q_recv, c_send, head_pad, ct_pad, q_ssem, q_rsem, c_ssem, c_rsem,
    qkv_t, dqkv_t, att_t,
    given, work, r0, r1, r2, rs_send, rs_recv, ag_send, ag_recv,
):
    plan = stages(dp, frame)
    bounds = chunk_bounds(given.shape[0], dp * frame)
    exchange(
        frame, plan, picked, patches, cot, gain, w_in, w_qkv, w_out, w_head,
        corr, w_in_t, w_qkv_t, w_out_t, ct, gain_col, d_y, datt_t,
        q_recv, c_send, head_pad, ct_pad, q_ssem, q_rsem, c_ssem, c_rsem,
    )
    ready, finish = device_sum(
        plan, bounds, given, summed, work, (r0, r1, r2), rs_send, rs_recv, ag_send, ag_recv
    )
    layer(
        corr, w_in_t, w_qkv_t, w_out_t, ct, gain_col, d_y, datt_t, w_qkv,
        given, qkv_t, dqkv_t, att_t, ready,
    )
    finish()


def train(dp, frame, rows, picked, patches, cot, gain, w_in, w_qkv, w_out, w_head):
    groups, fr_dev, cells, _ = patches.shape
    tracks, width = picked.shape
    hid = w_in.shape[1]
    tokens = cot.shape[1] * cot.shape[2]
    shape = (frame, groups // frame, fr_dev, tracks // groups, cells)
    vmem = pl.BlockSpec(memory_space=pltpu.VMEM)
    peers = pltpu.SemaphoreType.DMA((frame - 1,))
    scratch = [
        pltpu.VMEM(*item)
        for item in (
            (shape, BF16),
            (w_in.shape[::-1], BF16),
            (w_qkv.shape[::-1], BF16),
            (w_out.shape[::-1], BF16),
            ((PACK, tokens), BF16),
            ((hid, 1), F32),
            ((hid, tokens), F32),
            ((hid, tokens), BF16),
            ((frame - 1, tracks, width), BF16),
            (shape, BF16),
            ((PACK, hid), F32),
            ((PACK, tokens), F32),
        )
    ]
    scratch += [peers] * 4
    scratch += [
        pltpu.VMEM((3 * hid, tokens), BF16),
        pltpu.VMEM((3 * hid, tokens), BF16),
        pltpu.VMEM((hid, tokens), BF16),
    ]
    n_core, n_y, n_x, n_z = factors(dp, frame)
    sizes = (n_core, n_x * n_y, n_z)
    scratch += [pltpu.VMEM((rows, LANES), BF16)] * 2
    count = rows
    for size in sizes:
        count //= size
        scratch.append(pltpu.VMEM((max(size - 1, 1), count, LANES), BF16))
    chunks = len(chunk_bounds(rows, dp * frame))
    scratch += [pltpu.SemaphoreType.DMA((chunks, len(sizes), max(max(sizes) - 1, 1)))] * 4
    return pl.pallas_call(
        functools.partial(train_kernel, dp, frame),
        out_shape=jax.ShapeDtypeStruct((rows, LANES), BF16),
        in_specs=[vmem] * 8,
        out_specs=vmem,
        scratch_shapes=scratch,
        compiler_params=pltpu.CompilerParams(
            collective_id=0, has_side_effects=True, vmem_limit_bytes=48 * 2**20
        ),
        name="train",
    )(picked, patches, cot, gain, w_in, w_qkv, w_out, w_head)


def unpack_kernel(packed, g_in, g_gain, g_qkv, g_out, g_head):
    row = 0
    for ref in (g_out, g_qkv, g_in):
        height = ref.shape[0]
        for tile in range(ref.shape[1] // LANES):
            ref[:, tile * LANES : (tile + 1) * LANES] = packed[pl.ds(row, height), :].astype(F32)
            row += height
    for tile in range(g_head.shape[1] // LANES):
        small = packed[pl.ds(row, PACK), :].astype(F32)
        at = slice(tile * LANES, (tile + 1) * LANES)
        g_head[:, at] = small[0 : g_head.shape[0]]
        g_gain[at] = small[SUB]
        row += PACK


def unpack(packed, shapes):
    vmem = pl.BlockSpec(memory_space=pltpu.VMEM)
    return pl.pallas_call(
        unpack_kernel,
        out_shape=[jax.ShapeDtypeStruct(shape, F32) for shape in shapes],
        in_specs=[vmem],
        out_specs=[vmem] * len(shapes),
        compiler_params=pltpu.CompilerParams(vmem_limit_bytes=32 * 2**20),
        name="unpack",
    )(packed)


def body(
    dp,
    frame,
    features,
    vis_block,
    vis_count,
    query_frame,
    query_block,
    query_cell,
    cotangent,
    w_in,
    gain,
    w_qkv,
    w_out,
    w_head,
):
    hid = w_in.shape[1]
    cot = jnp.swapaxes(cotangent[0], 1, 2)
    picked, patches = pick(features, vis_block, vis_count, query_frame, query_block, query_cell)
    rows = packed_rows((w_in.shape, w_qkv.shape, w_out.shape, (PACK, hid)), dp * frame)
    summed = train(
        dp, frame, rows, picked, patches, cot, gain, w_in, w_qkv, w_out, w_head
    )
    return tuple(unpack(summed, (w_in.shape, gain.shape, w_qkv.shape, w_out.shape, w_head.shape)))


def solution(mesh):
    in_specs = (
        P("dp", "frame", None, None, None),
        P("dp", None, "frame", None),
        P("dp", None, "frame"),
        P("dp", None),
        P("dp", None),
        P("dp", None),
        P("dp", None, "frame", None),
        P(),
        P(),
        P(),
        P(),
        P(),
    )
    out_specs = (P(), P(), P(), P(), P())
    run = functools.partial(body, mesh.shape["dp"], mesh.shape["frame"])
    return jax.shard_map(run, mesh=mesh, in_specs=in_specs, out_specs=out_specs, check_vma=False)
```
